768 devices in a mesh: space: 12 (over z), help: 32 (over x, y), chan: 2 (over core).
Axes of the slice: x: 4, y: 8, z: 12, core: 2. Of those that a mesh axis runs over, the one named last changes fastest.
Arguments:
- node_feats: bfloat16 [12288, 49, 128], P(('space', 'help'), None, 'chan'), may hold values from -6 to 6
- source_index: int32 [1536, 128], P(('space', 'help')), may hold values from 0 to 287
- target_index: int32 [1536, 128], P(('space', 'help')), may hold values from 0 to 31
- edge_angle: float32 [1536, 128], P(('space', 'help')), may hold values from -3.140625 to 3.140625
- edge_envelope: float32 [1536, 128], P(('space', 'help')), may hold values from 0.1 to 1
- live_blocks: int32 [384], P(('space', 'help')), may hold values from 0 to 4, as said below
- w_zero: bfloat16 [7, 128, 896], replicated, may hold values from -0.1875 to 0.1875
- w_one: bfloat16 [2, 6, 128, 768], replicated, may hold values from -0.15625 to 0.15625
- w_two: bfloat16 [2, 5, 128, 640], replicated, may hold values from -0.15625 to 0.15625
Outputs:
- messages: bfloat16 [12288, 29, 128], P(('space', 'help'), None, 'chan')
The draws below stay inside these ranges and needn't reach their ends.
Inputs may be any that keep to these rules, and one draw needn't show every extreme that they name: A domain's live edge blocks are the first live_blocks of its 4 slots; edges in the other slots contribute nothing; some domain has all 4 live. `source_index`: index // 32 = 3 (ds + 1) + (dh + 1) names the domain at offset ds along space and dh along help, index % 32 an atom of it.
All inputs are finite; a program needn't handle non-finite values.
Results may differ from the reference program's by a relative error of at most 0.0065.
Values may be sent and summed in bfloat16 or wider, within the bound.
A program may use at most 64 MiB of HBM per device.

```python
import jax
import jax.numpy as jnp
import numpy as np
from jax import lax

C = 128
LMAX = 6
A_DEV = 32
NB = 4
EB = 128
COEF = 49
TRUNC = 29
ATOMS = 12288
BLOCKS = 1536
N_SPACE = 12
N_HELP = 32


def draw_live_blocks(key, part):
    domains = N_SPACE * N_HELP
    first_draw = jax.random.randint(jax.random.fold_in(key, 11), (domains,), 0, NB + 1)
    second_draw = jax.random.randint(jax.random.fold_in(key, 12), (domains,), 0, NB + 1)
    lowest = jnp.minimum(first_draw, second_draw)
    chosen = jax.random.randint(jax.random.fold_in(key, 13), (), 0, domains)
    return lowest.at[chosen].set(NB).astype(jnp.int32)


def with_ends(entries, key, smallest, top_value):
    dims = entries.shape
    index_at = [jax.random.randint(jax.random.fold_in(key, axis), (), 0, dims[axis]) for axis in range(len(dims))]
    entries = entries.at[tuple(index_at)].set(smallest)
    longest = dims.index(max(dims))
    index_at[longest] = (index_at[longest] + 1) % dims[longest]
    return entries.at[tuple(index_at)].set(top_value)


def block_scale(key, shape, cuts, low, largest):
    gain, own = 1.0, jax.random.fold_in(key, 6)
    for dim, blocks in cuts:
        heights = jnp.exp(jax.random.uniform(jax.random.fold_in(own, dim), (blocks,), jnp.float32, low / len(cuts), largest / len(cuts)))
        gain = gain * jnp.repeat(heights, shape[dim] // blocks).reshape([-1 if axis == dim else 1 for axis in range(len(shape))])
    return gain


def gaussian(stream_key, shape, scale, most, split=(), held_as=jnp.bfloat16):
    entries = scale * jax.random.normal(stream_key, shape, jnp.float32)
    if split:
        entries = entries * block_scale(stream_key, shape, split, -0.22, 0.18)
    return jnp.clip(entries, -most, most).astype(held_as)


def setup_inputs(seed: int = 0) -> dict:
    arg_keys = jax.random.split(jax.random.key(seed), 10)
    node_feats = gaussian(arg_keys[0], (ATOMS, COEF, C), 1.0, 6.0, ((0, 384), (2, 2)))
    source_index = with_ends(jax.random.randint(arg_keys[1], (BLOCKS, EB), 0, 9 * A_DEV), jax.random.fold_in(arg_keys[1], 1), 0, (9 * A_DEV) - 1).astype(jnp.int32)
    target_index = with_ends(jax.random.randint(arg_keys[2], (BLOCKS, EB), 0, A_DEV), jax.random.fold_in(arg_keys[2], 1), 0, A_DEV - 1).astype(jnp.int32)
    edge_angle = jnp.clip(jax.random.uniform(arg_keys[3], (BLOCKS, EB), jnp.float32, -3.140625, 3.140625), -3.140625, 3.140625)
    edge_envelope = jnp.clip(0.1 + 0.9 * jax.random.uniform(arg_keys[4], (BLOCKS, EB), jnp.float32) ** block_scale(arg_keys[4], (BLOCKS, EB), ((0, 384),), -0.2, 0.2), 0.1, 1.0)
    live_blocks = draw_live_blocks(jax.random.fold_in(arg_keys[9], 71), 0)
    w_zero = gaussian(arg_keys[6], (LMAX + 1, C, (LMAX + 1) * C), ((LMAX + 1) * C) ** -0.5, 0.1875)
    w_one = gaussian(arg_keys[7], (2, LMAX, C, LMAX * C), (2 * LMAX * C) ** -0.5, 0.15625)
    w_two = gaussian(arg_keys[8], (2, LMAX - 1, C, (LMAX - 1) * C), (2 * (LMAX - 1) * C) ** -0.5, 0.15625)
    return {"node_feats": node_feats, "source_index": source_index, "target_index": target_index, "edge_angle": edge_angle, "edge_envelope": edge_envelope, "live_blocks": live_blocks, "w_zero": w_zero, "w_one": w_one, "w_two": w_two}


def coefficient_order(top_degree):
    order_list = [degree * degree + degree for degree in range(top_degree + 1)]
    for order_m in (1, 2):
        order_list += [degree * degree + degree + order_m for degree in range(order_m, top_degree + 1)]
        order_list += [degree * degree + degree - order_m for degree in range(order_m, top_degree + 1)]
    return np.array(order_list, dtype=np.int32)


def turn_edges(features, edge_turn, direction, top_degree):
    count_zero, count_one, count_two = top_degree + 1, top_degree, top_degree - 1
    cos_one = jnp.cos(edge_turn)[:, None, None]
    sin_one = direction * jnp.sin(edge_turn)[:, None, None]
    cos_two = jnp.cos(2.0 * edge_turn)[:, None, None]
    sin_two = direction * jnp.sin(2.0 * edge_turn)[:, None, None]
    base_one = count_zero
    base_two = count_zero + 2 * count_one
    order_zero = features[:, :count_zero]
    plus_one = features[:, base_one:base_one + count_one]
    minus_one = features[:, base_one + count_one:base_two]
    plus_two = features[:, base_two:base_two + count_two]
    minus_two = features[:, base_two + count_two:]
    return jnp.concatenate([order_zero, cos_one * plus_one + sin_one * minus_one, cos_one * minus_one - sin_one * plus_one,
                            cos_two * plus_two + sin_two * minus_two, cos_two * minus_two - sin_two * plus_two], axis=1)


def mix_orders(rotated, weight_set, top_degree):
    count_zero, count_one, count_two = top_degree + 1, top_degree, top_degree - 1
    edge_count = rotated.shape[0]
    in_width = rotated.shape[2]
    zero_weight, one_real, one_imag, two_real, two_imag = weight_set
    out_width = zero_weight.shape[1] // count_zero

    def flatten(lower, upper):
        return rotated[:, lower:upper].reshape(edge_count, (upper - lower) * in_width)

    def product(left, right):
        return jnp.dot(left, right, preferred_element_type=jnp.float32)

    base_two = count_zero + 2 * count_one
    plus_one = flatten(count_zero, count_zero + count_one)
    minus_one = flatten(count_zero + count_one, base_two)
    plus_two = flatten(base_two, base_two + count_two)
    minus_two = flatten(base_two + count_two, base_two + 2 * count_two)
    pieces = [(product(flatten(0, count_zero), zero_weight), count_zero),
              (product(plus_one, one_real) - product(minus_one, one_imag), count_one),
              (product(plus_one, one_imag) + product(minus_one, one_real), count_one),
              (product(plus_two, two_real) - product(minus_two, two_imag), count_two),
              (product(plus_two, two_imag) + product(minus_two, two_real), count_two)]
    return jnp.concatenate([piece.reshape(edge_count, rows, out_width) for piece, rows in pieces], axis=1)


def reference(node_feats, source_index, target_index, edge_angle, edge_envelope, live_blocks, w_zero, w_one, w_two):
    order_list = coefficient_order(LMAX)
    cut_off = node_feats[:, order_list, :]
    domains = N_SPACE * N_HELP
    grid = cut_off.reshape(N_SPACE, N_HELP, A_DEV, TRUNC, C)
    padded = jnp.pad(grid, ((1, 1), (1, 1), (0, 0), (0, 0), (0, 0)))
    square = (LMAX + 1) * C
    weight_set = (w_zero.reshape(square, square),
                  w_one[0].reshape(LMAX * C, LMAX * C), w_one[1].reshape(LMAX * C, LMAX * C),
                  w_two[0].reshape((LMAX - 1) * C, (LMAX - 1) * C), w_two[1].reshape((LMAX - 1) * C, (LMAX - 1) * C))
    sources = source_index.reshape(domains, NB, EB)
    targets = target_index.reshape(domains, NB, EB)
    angles = edge_angle.reshape(domains, NB, EB)
    envelopes = edge_envelope.reshape(domains, NB, EB)

    def one_domain(domain):
        row_pos = (domain // N_HELP).astype(jnp.int32)
        col_pos = (domain % N_HELP).astype(jnp.int32)
        zero_pos = jnp.zeros((), jnp.int32)
        nearby = lax.dynamic_slice(padded, (row_pos, col_pos, zero_pos, zero_pos, zero_pos),
                                   (3, 3, A_DEV, TRUNC, C)).reshape(9 * A_DEV, TRUNC, C)

        def one_block(running, block_id):
            picked = nearby[sources[domain, block_id]]
            turn = angles[domain, block_id]
            rotated = turn_edges(picked.astype(jnp.float32), turn, 1.0, LMAX).astype(jnp.bfloat16)
            mixed = mix_orders(rotated, weight_set, LMAX)
            message = mixed * envelopes[domain, block_id][:, None, None]
            alive = (block_id < live_blocks[domain]).astype(jnp.float32)
            summed = jnp.zeros((A_DEV, TRUNC, C), jnp.float32).at[targets[domain, block_id]].add(message)
            return running + alive * summed, None

        running, unused = lax.scan(one_block, jnp.zeros((A_DEV, TRUNC, C), jnp.float32), jnp.arange(NB, dtype=jnp.int32))
        return running

    result = lax.map(one_domain, jnp.arange(domains, dtype=jnp.int32))
    return result.reshape(A_DEV * domains, TRUNC, C).astype(jnp.bfloat16)
```

```python
import functools

import jax
import jax.numpy as jnp
from jax import lax
from jax.experimental import pallas as pl
from jax.experimental.pallas import tpu as pltpu
from jax.sharding import PartitionSpec as P

MESH = pl.DeviceIdType.MESH
F32, BF16 = jnp.float32, jnp.bfloat16
ATOMS = 32
HALF = 64
ROW = 3 * ATOMS

PLUS_ONE = [l * l + l + 1 for l in range(1, 7)]
MINUS_ONE = [l * l + l - 1 for l in range(1, 7)]
PLUS_TWO = [l * l + l + 2 for l in range(2, 7)]
MINUS_TWO = [l * l + l - 2 for l in range(2, 7)]
ZERO = [l * l + l for l in range(7)]
PACK = (
    PLUS_ONE + MINUS_ONE,
    PLUS_TWO[:4] + MINUS_TWO[:4] + [PLUS_TWO[4], MINUS_TWO[4]],
    ZERO + ZERO[-1:],
)
WIDTH = tuple(HALF * len(order) for order in PACK)
SUMS = ((2 * ATOMS, 768), (2 * ATOMS, 640), (ATOMS, 896))
OUT_AT = ((7, 12), (19, 10), (0, 7))


def dot(a, b):
    return jnp.dot(a, b, preferred_element_type=F32)


def kernel(
    n_space, n_help,
    x_hbm, src_hbm, tgt_hbm, ang_hbm, env_hbm, live_hbm, w0_hbm, w1_hbm, w2_hbm,
    out_ref,
    src_ref, tgt_ref, ang_ref, env_ref, live_ref, xv, rx_one, rx_two, rx_zero, edges, edges_in,
    tx_one, tx_two, tx_zero, in_one, in_two, in_zero,
    wv_one, wv_two, wv_zero, give,
    in_sem, w_sem, halo_send, halo_recv, edge_send, edge_recv,
    sum_send, sum_recv, out_send, out_recv,
):
    s, h, c = lax.axis_index("space"), lax.axis_index("help"), lax.axis_index("chan")
    has_help = (h > 0, h < n_help - 1)
    has_space = (s > 0, s < n_space - 1)
    rx = (rx_one, rx_two, rx_zero)
    tx = (tx_one, tx_two, tx_zero)
    sums_in = (in_one, in_two, in_zero)
    partner = (s, h, 1 - c)

    barrier = pltpu.get_barrier_semaphore()

    def greet(device):
        pl.semaphore_signal(barrier, inc=1, device_id=device, device_id_type=MESH)

    greet(partner)
    for side in range(2):
        step = 2 * side - 1

        @pl.when(has_help[side])
        def _():
            greet((s, h + step, 0))
            greet((s, h + step, 1))

        @pl.when(has_space[side])
        def _():
            greet((s + step, h, c))

    loads = [
        pltpu.make_async_copy(source, held, in_sem.at[at])
        for at, (source, held) in enumerate((
            (x_hbm, xv), (src_hbm, src_ref), (tgt_hbm, tgt_ref), (ang_hbm, ang_ref),
            (env_hbm, env_ref), (live_hbm, live_ref),
        ))
    ]
    for load in loads:
        load.start()

    def weight_copies(role):
        if role == 0:
            return [
                pltpu.make_async_copy(
                    w1_hbm.at[part, :, pl.ds(half * HALF, HALF)], wv_one.at[part, half],
                    w_sem.at[2 * part + half],
                )
                for part in range(2) for half in range(2)
            ]
        copies = []
        for part in range(2):
            for half in range(2):
                copies.append(pltpu.make_async_copy(
                    w2_hbm.at[part, pl.ds(0, 4), pl.ds(half * HALF, HALF)],
                    wv_two.at[part, pl.ds(4 * half, 4)], w_sem.at[len(copies)],
                ))
            copies.append(pltpu.make_async_copy(
                w2_hbm.at[part, 4, pl.ds(0, HALF)], wv_two.at[part, 8], w_sem.at[len(copies)],
            ))
            copies.append(pltpu.make_async_copy(
                w2_hbm.at[part, 4, pl.ds(HALF, HALF)], wv_two.at[part, 9], w_sem.at[len(copies)],
            ))
        for half in range(2):
            copies.append(pltpu.make_async_copy(
                w0_hbm.at[pl.ds(0, 6), pl.ds(half * HALF, HALF)],
                wv_zero.at[pl.ds(6 * half, 6)], w_sem.at[len(copies)],
            ))
        for half in range(2):
            copies.append(pltpu.make_async_copy(
                w0_hbm.at[6, pl.ds(half * HALF, HALF)], wv_zero.at[12 + half],
                w_sem.at[len(copies)],
            ))
        return copies

    for load in loads[1:]:
        load.wait()
    block = lax.broadcasted_iota(jnp.int32, (4, 128), 0)
    angle = ang_ref[...]
    alive = jnp.where(block < live_ref[0], env_ref[...], 0.0)
    edges[0:4] = src_ref[...].astype(F32)
    edges[4:8] = tgt_ref[...].astype(F32)
    edges[8:12] = alive
    edges[12:16] = alive * jnp.cos(angle)
    edges[16:20] = alive * jnp.sin(angle)
    edges[20:24] = alive * jnp.cos(2.0 * angle)
    edges[24:28] = alive * jnp.sin(2.0 * angle)
    edges[28:32] = jnp.zeros((4, 128), F32)

    for side in range(2):

        @pl.when(jnp.logical_not(has_help[side]))
        def _():
            for ref, width in zip(rx, WIDTH):
                for half in range(2):
                    ref[half, 2 * side] = jnp.zeros((ATOMS, width), BF16)

        @pl.when(jnp.logical_not(has_space[side]))
        def _():
            edges_in[side] = jnp.zeros((32, 128), F32)
            for ref, (rows, width) in zip(sums_in, SUMS):
                ref[side] = jnp.zeros((rows, width), BF16)

    loads[0].wait()
    for ref, order in zip(rx, PACK):
        for pair in range(len(order) // 2):
            ref[c, 1, :, pl.ds(128 * pair, 128)] = jnp.concatenate(
                [xv[order[2 * pair]], xv[order[2 * pair + 1]]], axis=1
            )

    expected = 1
    for side in range(2):
        expected = expected + 2 * has_help[side].astype(jnp.int32) + has_space[side].astype(jnp.int32)
    pl.semaphore_wait(barrier, expected)

    def edge_copy(side):
        return pltpu.make_async_remote_copy(
            src_ref=edges, dst_ref=edges_in.at[1 - side],
            send_sem=edge_send.at[side], recv_sem=edge_recv.at[1 - side],
            device_id=(s + 2 * side - 1, h, c), device_id_type=MESH,
        )

    def halo_copy(plane, side):
        return pltpu.make_async_remote_copy(
            src_ref=rx[plane].at[c, 1], dst_ref=rx[plane].at[c, 2 - 2 * side],
            send_sem=halo_send.at[plane, 2 * side], recv_sem=halo_recv.at[plane, c, 2 - 2 * side],
            device_id=(s, h + 2 * side - 1, min(plane, 1)), device_id_type=MESH,
        )

    def pair_copy(plane):
        return pltpu.make_async_remote_copy(
            src_ref=rx[plane].at[c, 1], dst_ref=rx[plane].at[c, 1],
            send_sem=halo_send.at[plane, 1], recv_sem=halo_recv.at[plane, c, 1],
            device_id=partner, device_id_type=MESH,
        )

    def sum_copy(plane, side):
        return pltpu.make_async_remote_copy(
            src_ref=tx[plane].at[side], dst_ref=sums_in[plane].at[1 - side],
            send_sem=sum_send.at[plane, side], recv_sem=sum_recv.at[plane, 1 - side],
            device_id=(s + 2 * side - 1, h, c), device_id_type=MESH,
        )

    def out_copy(plane):
        at = pl.ds(*OUT_AT[plane])
        return pltpu.make_async_remote_copy(
            src_ref=give.at[at], dst_ref=out_ref.at[at],
            send_sem=out_send.at[plane], recv_sem=out_recv.at[plane],
            device_id=partner, device_id_type=MESH,
        )

    def arrived(dst, sem):
        pltpu.make_async_copy(dst, dst, sem).wait()

    for side in range(2):

        @pl.when(has_space[side])
        def _():
            edge_copy(side).start()

    for plane in range(3):
        for side in range(2):

            @pl.when(has_help[side])
            def _():
                halo_copy(plane, side).start()

        @pl.when(c != min(plane, 1))
        def _():
            pair_copy(plane).start()

    ids_row = lax.broadcasted_iota(jnp.int32, (ROW, 128), 0).astype(F32)
    ids_atom = lax.broadcasted_iota(jnp.int32, (ATOMS, 128), 0).astype(F32)

    def gathering(which, picks):
        held = edges if which == 1 else edges_in.at[which // 2]
        first = float(ROW * (2 - which))
        left, right = [], []
        for b in range(4):
            source = held[b:b + 1] - first
            target = held[4 + b:5 + b] == ids_atom
            right.append(jnp.where(source == ids_row, 1.0, 0.0).astype(BF16))
            left.append(jnp.concatenate(
                [jnp.where(target, held[pick + b:pick + b + 1], 0.0) for pick in picks], axis=0
            ).astype(BF16))
        return lax.dot_general(
            jnp.concatenate(left, axis=1), jnp.concatenate(right, axis=1),
            (((1,), (1,)), ((), ())), preferred_element_type=F32,
        ).astype(BF16)

    def all_gatherings(picks):
        middle = gathering(1, picks)
        for side in range(2):

            @pl.when(has_space[side])
            def _():
                arrived(edges_in.at[side], edge_recv.at[side])

        return [gathering(0, picks), middle, gathering(2, picks)]

    def wait_halo(plane, own):
        for half in range(2):
            for side in range(2):

                @pl.when(has_help[side])
                def _():
                    arrived(rx[plane].at[half, 2 * side], halo_recv.at[plane, half, 2 * side])

        arrived(rx[plane].at[1 - own, 1], halo_recv.at[plane, 1 - own, 1])

    def send_sums(plane):
        for side in range(2):

            @pl.when(has_space[side])
            def _():
                sum_copy(plane, side).start()

    def total(plane, own_part):
        for side in range(2):

            @pl.when(has_space[side])
            def _():
                arrived(sums_in[plane].at[side], sum_recv.at[plane, side])

        ref = sums_in[plane]
        return (own_part + ref[0].astype(F32) + ref[1].astype(F32)).astype(BF16)

    def finish(plane, own, pieces):
        row = OUT_AT[plane][0]
        for piece in pieces:
            rounded = piece.astype(BF16)
            for degree in range(piece.shape[1] // 128):
                lower = rounded[:, 128 * degree:128 * degree + HALF]
                upper = rounded[:, 128 * degree + HALF:128 * degree + 128]
                out_ref[row] = (lower, upper)[own]
                give[row] = (upper, lower)[own]
                row += 1
        out_copy(plane).start()

    def by_lane(a, b):
        low = lax.broadcasted_iota(jnp.int32, a.shape, 1) < HALF
        return (
            jnp.where(low, a, pltpu.roll(b, HALF, 1)),
            jnp.where(low, pltpu.roll(a, HALF, 1), b),
        )

    def rotated_mix(lhs, real, imag):
        by_real, by_imag = dot(lhs, real), dot(lhs, imag)
        return [by_real[:ATOMS] - by_imag[ATOMS:], by_imag[:ATOMS] + by_real[ATOMS:]]

    @pl.when(c == 0)
    def _():
        copies = weight_copies(0)
        for copy in copies:
            copy.start()
        turn = jnp.concatenate(all_gatherings((12, 16)), axis=0)
        wait_halo(0, 0)
        parts = [dot(turn, rx_one[half].reshape(ROW, 768)) for half in range(2)]
        own_sum = None
        for which in range(3):
            at = 2 * ATOMS * which
            plus, minus = [], []
            for part in parts:
                by_cos, by_sin = part[at:at + ATOMS], part[at + ATOMS:at + 2 * ATOMS]
                plus.append(by_cos[:, :384] + by_sin[:, 384:])
                minus.append(by_cos[:, 384:] - by_sin[:, :384])
            both = jnp.concatenate(
                [jnp.concatenate(plus, axis=1), jnp.concatenate(minus, axis=1)], axis=0
            )
            if which == 1:
                own_sum = both
            else:
                tx_one[which // 2] = both.astype(BF16)
        send_sums(0)
        for copy in copies:
            copy.wait()
        summed = total(0, own_sum)
        finish(0, 0, rotated_mix(
            summed, wv_one[0].reshape(768, 768), wv_one[1].reshape(768, 768)
        ))
        out_copy(0).wait_send()
        for plane in (1, 2):
            at = pl.ds(*OUT_AT[plane])
            arrived(out_ref.at[at], out_recv.at[plane])
        for side in range(2):

            @pl.when(has_space[side])
            def _():
                sum_copy(0, side).wait_send()

        for plane in (1, 2):
            pair_copy(plane).wait_send()

    @pl.when(c == 1)
    def _():
        copies = weight_copies(1)
        for copy in copies:
            copy.start()
        full = all_gatherings((20, 24, 8))
        turn = jnp.concatenate([each[:2 * ATOMS] for each in full], axis=0)
        flat = jnp.concatenate([each[2 * ATOMS:] for each in full], axis=0)
        wait_halo(1, 1)
        parts = [dot(turn, rx_two[half].reshape(ROW, 640)) for half in range(2)]
        own_two = None
        for which in range(3):
            at = 2 * ATOMS * which
            plus, minus, tails = [], [], []
            low = lax.broadcasted_iota(jnp.int32, (ATOMS, 128), 1) < HALF
            for part in parts:
                by_cos, by_sin = part[at:at + ATOMS], part[at + ATOMS:at + 2 * ATOMS]
                plus.append(by_cos[:, :256] + by_sin[:, 256:512])
                minus.append(by_cos[:, 256:512] - by_sin[:, :256])
                crossed = pltpu.roll(by_sin[:, 512:], HALF, 1)
                tails.append(by_cos[:, 512:] + jnp.where(low, crossed, -crossed))
            plus_tail, minus_tail = by_lane(*tails)
            both = jnp.concatenate([
                jnp.concatenate(plus + [plus_tail], axis=1),
                jnp.concatenate(minus + [minus_tail], axis=1),
            ], axis=0)
            if which == 1:
                own_two = both
            else:
                tx_two[which // 2] = both.astype(BF16)
        send_sums(1)
        wait_halo(2, 1)
        parts = [dot(flat, rx_zero[half].reshape(ROW, 512)) for half in range(2)]
        own_zero = None
        for which in range(3):
            at = ATOMS * which
            one, two = parts[0][at:at + ATOMS], parts[1][at:at + ATOMS]
            tail, _unused = by_lane(one[:, 384:], two[:, 384:])
            whole = jnp.concatenate([one[:, :384], two[:, :384], tail], axis=1)
            if which == 1:
                own_zero = whole
            else:
                tx_zero[which // 2] = whole.astype(BF16)
        send_sums(2)
        for copy in copies:
            copy.wait()
        summed = total(1, own_two)
        finish(1, 1, rotated_mix(
            summed, wv_two[0].reshape(640, 640), wv_two[1].reshape(640, 640)
        ))
        summed = total(2, own_zero)
        finish(2, 1, [dot(summed, wv_zero[...].reshape(896, 896))])
        for plane in (1, 2):
            out_copy(plane).wait_send()
        arrived(out_ref.at[pl.ds(*OUT_AT[0])], out_recv.at[0])
        for plane in (1, 2):
            for side in range(2):

                @pl.when(has_space[side])
                def _():
                    sum_copy(plane, side).wait_send()

        pair_copy(0).wait_send()

    for side in range(2):

        @pl.when(has_space[side])
        def _():
            edge_copy(side).wait_send()

        @pl.when(has_help[side])
        def _():
            for plane in range(3):
                halo_copy(plane, side).wait_send()


def solution(mesh):
    n_space, n_help = mesh.shape["space"], mesh.shape["help"]

    def shards(node_feats, source_index, target_index, edge_angle, edge_envelope, live_blocks,
               w_zero, w_one, w_two):
        feats = jnp.transpose(node_feats, (1, 0, 2))
        anywhere = pl.BlockSpec(memory_space=pltpu.HBM)
        in_vmem = pl.BlockSpec(memory_space=pltpu.VMEM)
        dma = pltpu.SemaphoreType.DMA
        out = pl.pallas_call(
            functools.partial(kernel, n_space, n_help),
            out_shape=jax.ShapeDtypeStruct((29, ATOMS, HALF), BF16),
            in_specs=[anywhere] * 9,
            out_specs=in_vmem,
            scratch_shapes=[
                pltpu.VMEM((4, 128), jnp.int32), pltpu.VMEM((4, 128), jnp.int32),
                pltpu.VMEM((4, 128), F32), pltpu.VMEM((4, 128), F32),
                pltpu.SMEM((1,), jnp.int32),
                pltpu.VMEM(feats.shape, BF16),
                *[pltpu.VMEM((2, 3, ATOMS, width), BF16) for width in WIDTH],
                pltpu.VMEM((32, 128), F32),
                pltpu.VMEM((2, 32, 128), F32),
                *[pltpu.VMEM((2, *shape), BF16) for shape in SUMS],
                *[pltpu.VMEM((2, *shape), BF16) for shape in SUMS],
                pltpu.VMEM((2, 2, 6, HALF, 768), BF16),
                pltpu.VMEM((2, 10, HALF, 640), BF16),
                pltpu.VMEM((14, HALF, 896), BF16),
                pltpu.VMEM((29, ATOMS, HALF), BF16),
                dma((6,)), dma((12,)), dma((3, 3)), dma((3, 2, 3)), dma((2,)), dma((2,)),
                dma((3, 2)), dma((3, 2)), dma((3,)), dma((3,)),
            ],
            compiler_params=pltpu.CompilerParams(
                collective_id=0, has_side_effects=True, vmem_limit_bytes=63 * 1024 * 1024
            ),
            cost_estimate=pl.CostEstimate(
                flops=2 * 64 * 3 * 1024 * 1024, bytes_accessed=8 * 1024 * 1024, transcendentals=2048
            ),
            name="edge_mix",
        )(feats, source_index, target_index, edge_angle, edge_envelope, live_blocks,
          w_zero, w_one, w_two)
        return jnp.transpose(out, (1, 0, 2))

    return jax.shard_map(
        shards,
        mesh=mesh,
        in_specs=(
            P(("space", "help"), None, "chan"),
            P(("space", "help"), None),
            P(("space", "help"), None),
            P(("space", "help"), None),
            P(("space", "help"), None),
            P(("space", "help")),
            P(), P(), P(),
        ),
        out_specs=P(("space", "help"), None, "chan"),
        check_vma=False,
    )
```

```python
import functools

import jax
import jax.numpy as jnp
from jax import lax
from jax.experimental import pallas as pl
from jax.experimental.pallas import tpu as pltpu
from jax.sharding import PartitionSpec as P

MESH = pl.DeviceIdType.MESH
F32, BF16 = jnp.float32, jnp.bfloat16
ATOMS = 32
HALF = 64
ROW = 3 * ATOMS

PLUS_ONE = [l * l + l + 1 for l in range(1, 7)]
MINUS_ONE = [l * l + l - 1 for l in range(1, 7)]
PLUS_TWO = [l * l + l + 2 for l in range(2, 7)]
MINUS_TWO = [l * l + l - 2 for l in range(2, 7)]
ZERO = [l * l + l for l in range(7)]
PACK = (
    PLUS_ONE + MINUS_ONE,
    PLUS_TWO[:4] + MINUS_TWO[:4] + [PLUS_TWO[4], MINUS_TWO[4]],
    ZERO + ZERO[-1:],
)
WIDTH = tuple(HALF * len(order) for order in PACK)
RUNS = [(0, 4)] + [(l * l + l - 2, 5) for l in range(2, 7)]
OUT_AT = ((7, 12), (19, 10), (0, 7))
GIVEN = (768, 640, 512)
COS_ONE, SIN_ONE, SOURCE, TARGET, COS_TWO, SIN_TWO, PLAIN = range(0, 28, 4)
EDGE_ROWS = (None, (0, 32))
FIRST = (0, 0, 0)


def dot(a, b):
    return jnp.dot(a, b, preferred_element_type=F32)


def kernel(
    n_space, n_help,
    x_hbm, src_hbm, tgt_hbm, ang_hbm, env_hbm, live_hbm, w0_hbm, w1_hbm, w2_hbm,
    out_ref,
    src_ref, tgt_ref, ang_ref, env_ref, live_ref, xv, rx_one, rx_two, rx_zero, edges, edges_in,
    tx_one, tx_two, tx_zero, in_one, in_two, in_zero,
    wv_one, wv_two, wv_zero, give_one, give_two, give_zero, take_one, take_two, take_zero,
    x_sem, in_sem, w_sem, halo_send, halo_recv, edge_send, edge_recv,
    sum_send, sum_recv, out_send, out_recv,
):
    s, h, c = lax.axis_index("space"), lax.axis_index("help"), lax.axis_index("chan")
    has = ((h > 0, h < n_help - 1), (s > 0, s < n_space - 1))
    rx = (rx_one, rx_two, rx_zero)
    tx = (tx_one, tx_two, tx_zero)
    sums_in = (in_one, in_two, in_zero)
    give = (give_one, give_two, give_zero)
    take = (take_one, take_two, take_zero)
    partner = (s, h, 1 - c)

    def neighbour(axis, side):
        step = 2 * side - 1
        return (s, h + step, c) if axis == 0 else (s + step, h, c)

    barrier = pltpu.get_barrier_semaphore()

    def greet(device):
        pl.semaphore_signal(barrier, inc=1, device_id=device, device_id_type=MESH)

    x_loads = [
        pltpu.make_async_copy(x_hbm.at[pl.ds(*run)], xv.at[pl.ds(*run)], x_sem.at[at])
        for at, run in enumerate(RUNS)
    ]
    loads = [
        pltpu.make_async_copy(source, held, in_sem.at[at])
        for at, (source, held) in enumerate((
            (src_hbm, src_ref), (tgt_hbm, tgt_ref), (ang_hbm, ang_ref),
            (env_hbm, env_ref), (live_hbm, live_ref),
        ))
    ]
    mine = pl.ds(pl.multiple_of(c * HALF, HALF), HALF)
    weights = [
        pltpu.make_async_copy(w1_hbm.at[:, :, mine], wv_one, w_sem.at[0]),
        pltpu.make_async_copy(w2_hbm.at[:, :, mine], wv_two, w_sem.at[1]),
        pltpu.make_async_copy(w0_hbm.at[:, mine], wv_zero, w_sem.at[2]),
    ]
    for load in x_loads:
        load.start()

    expected = 1
    for axis in range(2):
        for side in range(2):
            expected = expected + has[axis][side].astype(jnp.int32)

            @pl.when(has[axis][side])
            def _():
                greet(neighbour(axis, side))

    greet(partner)

    for load in loads:
        load.start()

    for axis in range(2):
        for side in range(2):

            @pl.when(jnp.logical_not(has[axis][side]))
            def _():
                edges_in[2 * axis + side] = jnp.zeros((32, 128), F32)
                for plane in range(3):
                    if FIRST[plane] == axis:
                        rx[plane][2 * side] = jnp.zeros((ATOMS, WIDTH[plane]), BF16)
                    else:
                        sums_in[plane][side] = jnp.zeros((ATOMS, WIDTH[plane]), BF16)

    def halo_copy(plane, side):
        return pltpu.make_async_remote_copy(
            src_ref=rx[plane].at[1], dst_ref=rx[plane].at[2 - 2 * side],
            send_sem=halo_send.at[plane, side], recv_sem=halo_recv.at[plane, 1 - side],
            device_id=neighbour(FIRST[plane], side), device_id_type=MESH,
        )

    def edge_copy(axis, side):
        rows = pl.ds(*EDGE_ROWS[axis])
        return pltpu.make_async_remote_copy(
            src_ref=edges.at[rows], dst_ref=edges_in.at[2 * axis + 1 - side, rows],
            send_sem=edge_send.at[axis, side], recv_sem=edge_recv.at[axis, 1 - side],
            device_id=neighbour(axis, side), device_id_type=MESH,
        )

    def sum_copy(plane, side):
        return pltpu.make_async_remote_copy(
            src_ref=tx[plane].at[side], dst_ref=sums_in[plane].at[1 - side],
            send_sem=sum_send.at[plane, side], recv_sem=sum_recv.at[plane, 1 - side],
            device_id=neighbour(1 - FIRST[plane], side), device_id_type=MESH,
        )

    def out_copy(plane):
        return pltpu.make_async_remote_copy(
            src_ref=give[plane], dst_ref=take[plane],
            send_sem=out_send.at[plane], recv_sem=out_recv.at[plane],
            device_id=partner, device_id_type=MESH,
        )

    for load in loads:
        load.wait()
    block = lax.broadcasted_iota(jnp.int32, (4, 128), 0)
    angle = ang_ref[...]
    alive = jnp.where(block < live_ref[0], env_ref[...], 0.0)
    for row, value in (
        (COS_ONE, alive * jnp.cos(angle)), (SIN_ONE, alive * jnp.sin(angle)),
        (SOURCE, src_ref[...].astype(F32)), (TARGET, tgt_ref[...].astype(F32)),
        (COS_TWO, alive * jnp.cos(2.0 * angle)), (SIN_TWO, alive * jnp.sin(2.0 * angle)),
        (PLAIN, alive), (PLAIN + 4, jnp.zeros((4, 128), F32)),
    ):
        edges[row:row + 4] = value
    for load in x_loads:
        load.wait()
    for plane, (ref, order) in enumerate(zip(rx, PACK)):
        for pair in range(len(order) // 2):
            ref[1, :, pl.ds(128 * pair, 128)] = jnp.concatenate(
                [xv[order[2 * pair]], xv[order[2 * pair + 1]]], axis=1
            )
        if plane == 0:
            pl.semaphore_wait(barrier, expected)
            for axis in (1,):
                for side in range(2):

                    @pl.when(has[axis][side])
                    def _():
                        edge_copy(axis, side).start()
        for side in range(2):

            @pl.when(has[FIRST[plane]][side])
            def _():
                halo_copy(plane, side).start()

    for load in weights:
        load.start()

    line = lax.broadcasted_iota(jnp.int32, (ROW, 128), 0)
    along_help = line.astype(F32)
    along_space = (line + 2 * ATOMS * (line // ATOMS)).astype(F32)
    ids_atom = lax.broadcasted_iota(jnp.int32, (ATOMS, 128), 0).astype(F32)

    def gathering(axis, which, picks):
        held = edges if which == 1 else edges_in.at[2 * (1 - axis) + which // 2]
        names = along_help if axis == 0 else along_space
        first = float((2 - which) * (ROW if axis == 0 else ATOMS))
        left, right = [], []
        for b in range(4):
            source = held[SOURCE + b:SOURCE + b + 1] - first
            target = held[TARGET + b:TARGET + b + 1] == ids_atom
            right.append(jnp.where(source == names, 1.0, 0.0).astype(BF16))
            left.append(jnp.concatenate(
                [jnp.where(target, held[at + b:at + b + 1], 0.0) for at in picks], axis=0
            ).astype(BF16))
        return lax.dot_general(
            jnp.concatenate(left, axis=1), jnp.concatenate(right, axis=1),
            (((1,), (1,)), ((), ())), preferred_element_type=F32,
        ).astype(BF16)

    picks = (COS_ONE, SIN_ONE, COS_TWO, SIN_TWO, PLAIN)
    middle = gathering(0, 1, picks)
    for side in range(2):

        @pl.when(has[1][side])
        def _():
            edge_copy(1, 1 - side).wait_recv()

    full = [gathering(0, 0, picks), middle, gathering(0, 2, picks)]
    lhs = [
        jnp.concatenate([each[first:first + rows] for each in full], axis=0)
        for first, rows in ((0, 2 * ATOMS), (2 * ATOMS, 2 * ATOMS), (4 * ATOMS, ATOMS))
    ]
    low = lax.broadcasted_iota(jnp.int32, (ATOMS, 128), 1) < HALF

    def turned(plane, part):
        if plane == 2:
            return part
        by_cos, by_sin = part[:ATOMS], part[ATOMS:]
        if plane == 0:
            return jnp.concatenate([
                by_cos[:, :384] + by_sin[:, 384:], by_cos[:, 384:] - by_sin[:, :384]
            ], axis=1)
        crossed = pltpu.roll(by_sin[:, 512:], HALF, 1)
        return jnp.concatenate([
            by_cos[:, :256] + by_sin[:, 256:512],
            by_cos[:, 256:512] - by_sin[:, :256],
            by_cos[:, 512:] + jnp.where(low, crossed, -crossed),
        ], axis=1)

    own = []
    for plane in range(3):
        for side in range(2):

            @pl.when(has[FIRST[plane]][side])
            def _():
                halo_copy(plane, 1 - side).wait_recv()

        part = dot(lhs[plane], rx[plane][...].reshape(ROW, WIDTH[plane]))
        rows = part.shape[0] // 3
        for side in range(2):
            tx[plane][side] = turned(plane, part[2 * side * rows:(2 * side + 1) * rows]).astype(BF16)

            @pl.when(has[1 - FIRST[plane]][side])
            def _():
                sum_copy(plane, side).start()

        own.append(turned(plane, part[rows:2 * rows]))

    for axis in range(2):
        for side in range(2):

            @pl.when(has[axis][side])
            def _():
                if axis == 1:
                    edge_copy(axis, side).wait_send()
                for plane in range(3):
                    if FIRST[plane] == axis:
                        halo_copy(plane, side).wait_send()

    for load in weights:
        load.wait()

    def by_lane(a, b):
        return (
            jnp.where(low, a, pltpu.roll(b, HALF, 1)),
            jnp.where(low, pltpu.roll(a, HALF, 1), b),
        )

    def rotated_mix(sums, real, imag):
        by_real, by_imag = dot(sums, real), dot(sums, imag)
        return [by_real[:ATOMS] - by_imag[ATOMS:], by_imag[:ATOMS] + by_real[ATOMS:]]

    first_core = c == 0
    kept = []
    for plane in range(3):
        for side in range(2):

            @pl.when(has[1 - FIRST[plane]][side])
            def _():
                sum_copy(plane, 1 - side).wait_recv()

        y = own[plane] + sums_in[plane][0].astype(F32) + sums_in[plane][1].astype(F32)
        if plane == 0:
            mixed = rotated_mix(
                jnp.concatenate([y[:, :384], y[:, 384:]], axis=0).astype(BF16),
                wv_one[0].reshape(384, 768), wv_one[1].reshape(384, 768),
            )
        elif plane == 1:
            tail = y[:, 512:]
            mixed = rotated_mix(
                jnp.concatenate([
                    jnp.concatenate([y[:, :256], tail], axis=1),
                    jnp.concatenate([y[:, 256:512], pltpu.roll(tail, HALF, 1)], axis=1),
                ], axis=0).astype(BF16)[:, :320],
                wv_two[0].reshape(320, 640), wv_two[1].reshape(320, 640),
            )
        else:
            mixed = [dot(y[:, :448].astype(BF16), wv_zero[...].reshape(448, 896))]
        blocks = [
            piece[:, 128 * degree:128 * degree + 128]
            for piece in mixed for degree in range(piece.shape[1] // 128)
        ]
        keep = []
        for pair in range((len(blocks) + 1) // 2):
            lower, upper = by_lane(blocks[2 * pair], blocks[min(2 * pair + 1, len(blocks) - 1)])
            keep.append(jnp.where(first_core, lower, upper))
            give[plane][:, pl.ds(128 * pair, 128)] = jnp.where(first_core, upper, lower).astype(BF16)
        kept.append(keep)
        out_copy(plane).start()

    for plane in range(3):
        for side in range(2):

            @pl.when(has[1 - FIRST[plane]][side])
            def _():
                sum_copy(plane, side).wait_send()

    for plane in range(3):
        out_copy(plane).wait_recv()
        row, count = OUT_AT[plane]
        for pair, keep in enumerate(kept[plane]):
            whole = (keep + take[plane][:, pl.ds(128 * pair, 128)].astype(F32)).astype(BF16)
            out_ref[row + 2 * pair] = whole[:, :HALF]
            if 2 * pair + 1 < count:
                out_ref[row + 2 * pair + 1] = whole[:, HALF:]

    for plane in range(3):
        out_copy(plane).wait_send()


def solution(mesh):
    n_space, n_help = mesh.shape["space"], mesh.shape["help"]

    def shards(node_feats, source_index, target_index, edge_angle, edge_envelope, live_blocks,
               w_zero, w_one, w_two):
        feats = jnp.transpose(node_feats, (1, 0, 2))
        anywhere = pl.BlockSpec(memory_space=pltpu.HBM)
        in_vmem = pl.BlockSpec(memory_space=pltpu.VMEM)
        dma = pltpu.SemaphoreType.DMA
        out = pl.pallas_call(
            functools.partial(kernel, n_space, n_help),
            out_shape=pltpu.VMEM((29, ATOMS, HALF), BF16),
            in_specs=[anywhere] * 9,
            out_specs=in_vmem,
            scratch_shapes=[
                pltpu.VMEM((4, 128), jnp.int32), pltpu.VMEM((4, 128), jnp.int32),
                pltpu.VMEM((4, 128), F32), pltpu.VMEM((4, 128), F32),
                pltpu.SMEM((1,), jnp.int32),
                pltpu.VMEM(feats.shape, BF16),
                *[pltpu.VMEM((3, ATOMS, width), BF16) for width in WIDTH],
                pltpu.VMEM((32, 128), F32),
                pltpu.VMEM((4, 32, 128), F32),
                *[pltpu.VMEM((2, ATOMS, width), BF16) for width in WIDTH + WIDTH],
                pltpu.VMEM((2, 6, HALF, 768), BF16),
                pltpu.VMEM((2, 5, HALF, 640), BF16),
                pltpu.VMEM((7, HALF, 896), BF16),
                *[pltpu.VMEM((ATOMS, width), BF16) for width in GIVEN + GIVEN],
                dma((6,)), dma((5,)), dma((3,)), dma((3, 2)), dma((3, 2)), dma((2, 2)), dma((2, 2)),
                dma((3, 2)), dma((3, 2)), dma((3,)), dma((3,)),
            ],
            compiler_params=pltpu.CompilerParams(
                collective_id=0, has_side_effects=True, vmem_limit_bytes=60 * 1024 * 1024
            ),
            cost_estimate=pl.CostEstimate(
                flops=2 * 64 * 3 * 1024 * 1024, bytes_accessed=8 * 1024 * 1024, transcendentals=2048
            ),
            name="edge_mix",
        )(feats, source_index, target_index, edge_angle, edge_envelope, live_blocks,
          w_zero, w_one, w_two)
        return jnp.transpose(out, (1, 0, 2))

    return jax.shard_map(
        shards,
        mesh=mesh,
        in_specs=(
            P(("space", "help"), None, "chan"),
            P(("space", "help"), None),
            P(("space", "help"), None),
            P(("space", "help"), None),
            P(("space", "help"), None),
            P(("space", "help")),
            P(), P(), P(),
        ),
        out_specs=P(("space", "help"), None, "chan"),
        check_vma=False,
    )
```

```python
import functools

import jax
import jax.numpy as jnp
from jax import lax
from jax.experimental import pallas as pl
from jax.experimental.pallas import tpu as pltpu
from jax.sharding import PartitionSpec as P

MESH = pl.DeviceIdType.MESH
F32, BF16 = jnp.float32, jnp.bfloat16
ATOMS = 32
HALF = 64
ROW = 3 * ATOMS

PLUS_ONE = [l * l + l + 1 for l in range(1, 7)]
MINUS_ONE = [l * l + l - 1 for l in range(1, 7)]
PLUS_TWO = [l * l + l + 2 for l in range(2, 7)]
MINUS_TWO = [l * l + l - 2 for l in range(2, 7)]
ZERO = [l * l + l for l in range(7)]
PACK = (
    PLUS_ONE + MINUS_ONE,
    PLUS_TWO[:4] + MINUS_TWO[:4] + [PLUS_TWO[4], MINUS_TWO[4]],
    ZERO + ZERO[-1:],
)
WIDTH = tuple(HALF * len(order) for order in PACK)
RUNS = [(0, 4)] + [(l * l + l - 2, 5) for l in range(2, 7)]
OUT_AT = ((7, 12), (19, 10), (0, 7))
GIVEN = (768, 640, 512)
COS_ONE, SIN_ONE, COS_TWO, SIN_TWO, PLAIN = range(0, 20, 4)
FIRST = (0, 0, 0)


def dot(a, b):
    return jnp.dot(a, b, preferred_element_type=F32)


def kernel(
    n_space, n_help,
    x_hbm, src_hbm, tgt_hbm, ang_hbm, env_hbm, live_ref, w0_hbm, w1_hbm, w2_hbm,
    out_ref,
    src_ref, tgt_ref, ang_ref, env_ref, live_at, xv, rx_one, rx_two, rx_zero, edges,
    tx_one, tx_two, tx_zero, in_one, in_two, in_zero,
    wv_one, wv_two, wv_zero, give_one, give_two, give_zero, take_one, take_two, take_zero,
    x_sem, in_sem, w_sem, halo_send, halo_recv, edge_send, edge_recv,
    sum_send, sum_recv, out_send, out_recv,
):
    s, h, c = lax.axis_index("space"), lax.axis_index("help"), lax.axis_index("chan")
    has = ((h > 0, h < n_help - 1), (s > 0, s < n_space - 1))
    rx = (rx_one, rx_two, rx_zero)
    tx = (tx_one, tx_two, tx_zero)
    sums_in = (in_one, in_two, in_zero)
    give = (give_one, give_two, give_zero)
    take = (take_one, take_two, take_zero)
    partner = (s, h, 1 - c)

    def neighbour(axis, side):
        step = 2 * side - 1
        return (s, h + step, c) if axis == 0 else (s + step, h, c)

    barrier = pltpu.get_barrier_semaphore()

    def greet(device):
        pl.semaphore_signal(barrier, inc=1, device_id=device, device_id_type=MESH)

    x_loads = [
        pltpu.make_async_copy(x_hbm.at[pl.ds(*run)], xv.at[pl.ds(*run)], x_sem.at[at])
        for at, run in enumerate(RUNS)
    ]
    raw_hbm = (src_hbm, tgt_hbm, ang_hbm, env_hbm)
    raw = (src_ref, tgt_ref, ang_ref, env_ref, live_at)
    loads = [
        pltpu.make_async_copy(source, held.at[1], in_sem.at[at])
        for at, (source, held) in enumerate(zip(raw_hbm, raw))
    ]
    mine = pl.ds(pl.multiple_of(c * HALF, HALF), HALF)
    weights = [
        pltpu.make_async_copy(w1_hbm.at[:, :, mine], wv_one, w_sem.at[0]),
        pltpu.make_async_copy(w2_hbm.at[:, :, mine], wv_two, w_sem.at[1]),
        pltpu.make_async_copy(w0_hbm.at[:, mine], wv_zero, w_sem.at[2]),
    ]
    for load in x_loads:
        load.start()

    expected = 1
    for axis in range(2):
        for side in range(2):
            expected = expected + has[axis][side].astype(jnp.int32)

            @pl.when(has[axis][side])
            def _():
                greet(neighbour(axis, side))

    greet(partner)

    for load in loads:
        load.start()

    live_at[1] = jnp.full((8, 128), live_ref[0], jnp.int32)

    for axis in range(2):
        for side in range(2):

            @pl.when(jnp.logical_not(has[axis][side]))
            def _():
                if axis == 1:
                    for ref in raw:
                        ref[2 * side] = jnp.zeros(ref.shape[1:], ref.dtype)
                for plane in range(3):
                    if FIRST[plane] == axis:
                        rx[plane][2 * side] = jnp.zeros((ATOMS, WIDTH[plane]), BF16)
                    else:
                        sums_in[plane][side] = jnp.zeros((ATOMS, WIDTH[plane]), BF16)

    def halo_copy(plane, side):
        return pltpu.make_async_remote_copy(
            src_ref=rx[plane].at[1], dst_ref=rx[plane].at[2 - 2 * side],
            send_sem=halo_send.at[plane, side], recv_sem=halo_recv.at[plane, 1 - side],
            device_id=neighbour(FIRST[plane], side), device_id_type=MESH,
        )

    def edge_copies(side):
        return [
            pltpu.make_async_remote_copy(
                src_ref=held.at[1] if at == 4 else raw_hbm[at], dst_ref=held.at[2 - 2 * side],
                send_sem=edge_send.at[side, at], recv_sem=edge_recv.at[1 - side, at],
                device_id=neighbour(1, side), device_id_type=MESH,
            )
            for at, held in enumerate(raw)
        ]

    def sum_copy(plane, side):
        return pltpu.make_async_remote_copy(
            src_ref=tx[plane].at[side], dst_ref=sums_in[plane].at[1 - side],
            send_sem=sum_send.at[plane, side], recv_sem=sum_recv.at[plane, 1 - side],
            device_id=neighbour(1 - FIRST[plane], side), device_id_type=MESH,
        )

    def out_copy(plane):
        return pltpu.make_async_remote_copy(
            src_ref=give[plane], dst_ref=take[plane],
            send_sem=out_send.at[plane], recv_sem=out_recv.at[plane],
            device_id=partner, device_id_type=MESH,
        )

    pl.semaphore_wait(barrier, expected)
    for side in range(2):

        @pl.when(has[1][side])
        def _():
            for copy in edge_copies(side):
                copy.start()

    for load in x_loads:
        load.wait()
    for plane, (ref, order) in enumerate(zip(rx, PACK)):
        for pair in range(len(order) // 2):
            ref[1, :, pl.ds(128 * pair, 128)] = jnp.concatenate(
                [xv[order[2 * pair]], xv[order[2 * pair + 1]]], axis=1
            )
        for side in range(2):

            @pl.when(has[FIRST[plane]][side])
            def _():
                halo_copy(plane, side).start()

    for load in weights:
        load.start()

    ids_row = lax.broadcasted_iota(jnp.int32, (ROW, 128), 0)
    ids_atom = lax.broadcasted_iota(jnp.int32, (ATOMS, 128), 0)
    block = lax.broadcasted_iota(jnp.int32, (4, 128), 0)

    def weigh(which):
        angle = ang_ref[which]
        alive = jnp.where(block < live_at[which, 0:4], env_ref[which], 0.0)
        for row, value in (
            (COS_ONE, alive * jnp.cos(angle)), (SIN_ONE, alive * jnp.sin(angle)),
            (COS_TWO, alive * jnp.cos(2.0 * angle)), (SIN_TWO, alive * jnp.sin(2.0 * angle)),
            (PLAIN, alive),
        ):
            edges[which, row:row + 4] = value

    def gathering(which):
        left, right = [], []
        for b in range(4):
            source = src_ref[which, b:b + 1] - ROW * (2 - which)
            target = tgt_ref[which, b:b + 1] == ids_atom
            right.append(jnp.where(source == ids_row, 1.0, 0.0).astype(BF16))
            left.append(jnp.concatenate([
                jnp.where(target, edges[which, at + b:at + b + 1], 0.0)
                for at in (COS_ONE, SIN_ONE, COS_TWO, SIN_TWO, PLAIN)
            ], axis=0).astype(BF16))
        return lax.dot_general(
            jnp.concatenate(left, axis=1), jnp.concatenate(right, axis=1),
            (((1,), (1,)), ((), ())), preferred_element_type=F32,
        ).astype(BF16)

    for load in loads:
        load.wait()
    weigh(1)
    middle = gathering(1)
    for side in range(2):

        @pl.when(has[1][side])
        def _():
            for copy in edge_copies(1 - side):
                copy.wait_recv()

        weigh(2 * side)
    full = [gathering(0), middle, gathering(2)]
    lhs = [
        jnp.concatenate([each[first:first + rows] for each in full], axis=0)
        for first, rows in ((0, 2 * ATOMS), (2 * ATOMS, 2 * ATOMS), (4 * ATOMS, ATOMS))
    ]
    low = lax.broadcasted_iota(jnp.int32, (ATOMS, 128), 1) < HALF

    def turned(plane, part):
        if plane == 2:
            return part
        by_cos, by_sin = part[:ATOMS], part[ATOMS:]
        if plane == 0:
            return jnp.concatenate([
                by_cos[:, :384] + by_sin[:, 384:], by_cos[:, 384:] - by_sin[:, :384]
            ], axis=1)
        crossed = pltpu.roll(by_sin[:, 512:], HALF, 1)
        return jnp.concatenate([
            by_cos[:, :256] + by_sin[:, 256:512],
            by_cos[:, 256:512] - by_sin[:, :256],
            by_cos[:, 512:] + jnp.where(low, crossed, -crossed),
        ], axis=1)

    own = []
    for plane in range(3):
        for side in range(2):

            @pl.when(has[FIRST[plane]][side])
            def _():
                halo_copy(plane, 1 - side).wait_recv()

        part = dot(lhs[plane], rx[plane][...].reshape(ROW, WIDTH[plane]))
        rows = part.shape[0] // 3
        for side in range(2):
            tx[plane][side] = turned(plane, part[2 * side * rows:(2 * side + 1) * rows]).astype(BF16)

            @pl.when(has[1 - FIRST[plane]][side])
            def _():
                sum_copy(plane, side).start()

        own.append(turned(plane, part[rows:2 * rows]))

    for axis in range(2):
        for side in range(2):

            @pl.when(has[axis][side])
            def _():
                if axis == 1:
                    for copy in edge_copies(side):
                        copy.wait_send()
                for plane in range(3):
                    if FIRST[plane] == axis:
                        halo_copy(plane, side).wait_send()

    for load in weights:
        load.wait()

    def by_lane(a, b):
        return (
            jnp.where(low, a, pltpu.roll(b, HALF, 1)),
            jnp.where(low, pltpu.roll(a, HALF, 1), b),
        )

    def rotated_mix(sums, real, imag):
        by_real, by_imag = dot(sums, real), dot(sums, imag)
        return [by_real[:ATOMS] - by_imag[ATOMS:], by_imag[:ATOMS] + by_real[ATOMS:]]

    first_core = c == 0
    kept = []
    for plane in range(3):
        for side in range(2):

            @pl.when(has[1 - FIRST[plane]][side])
            def _():
                sum_copy(plane, 1 - side).wait_recv()

        y = own[plane] + sums_in[plane][0].astype(F32) + sums_in[plane][1].astype(F32)
        if plane == 0:
            mixed = rotated_mix(
                jnp.concatenate([y[:, :384], y[:, 384:]], axis=0).astype(BF16),
                wv_one[0].reshape(384, 768), wv_one[1].reshape(384, 768),
            )
        elif plane == 1:
            tail = y[:, 512:]
            mixed = rotated_mix(
                jnp.concatenate([
                    jnp.concatenate([y[:, :256], tail], axis=1),
                    jnp.concatenate([y[:, 256:512], pltpu.roll(tail, HALF, 1)], axis=1),
                ], axis=0).astype(BF16)[:, :320],
                wv_two[0].reshape(320, 640), wv_two[1].reshape(320, 640),
            )
        else:
            mixed = [dot(y[:, :448].astype(BF16), wv_zero[...].reshape(448, 896))]
        blocks = [
            piece[:, 128 * degree:128 * degree + 128]
            for piece in mixed for degree in range(piece.shape[1] // 128)
        ]
        keep = []
        for pair in range((len(blocks) + 1) // 2):
            lower, upper = by_lane(blocks[2 * pair], blocks[min(2 * pair + 1, len(blocks) - 1)])
            keep.append(jnp.where(first_core, lower, upper))
            give[plane][:, pl.ds(128 * pair, 128)] = jnp.where(first_core, upper, lower).astype(BF16)
        kept.append(keep)
        out_copy(plane).start()

    for plane in range(3):
        for side in range(2):

            @pl.when(has[1 - FIRST[plane]][side])
            def _():
                sum_copy(plane, side).wait_send()

    for plane in range(3):
        out_copy(plane).wait_recv()
        row, count = OUT_AT[plane]
        for pair, keep in enumerate(kept[plane]):
            whole = (keep + take[plane][:, pl.ds(128 * pair, 128)].astype(F32)).astype(BF16)
            out_ref[row + 2 * pair] = whole[:, :HALF]
            if 2 * pair + 1 < count:
                out_ref[row + 2 * pair + 1] = whole[:, HALF:]

    for plane in range(3):
        out_copy(plane).wait_send()


def solution(mesh):
    n_space, n_help = mesh.shape["space"], mesh.shape["help"]

    def shards(node_feats, source_index, target_index, edge_angle, edge_envelope, live_blocks,
               w_zero, w_one, w_two):
        feats = jnp.transpose(node_feats, (1, 0, 2))
        anywhere = pl.BlockSpec(memory_space=pltpu.HBM)
        in_vmem = pl.BlockSpec(memory_space=pltpu.VMEM)
        dma = pltpu.SemaphoreType.DMA
        out = pl.pallas_call(
            functools.partial(kernel, n_space, n_help),
            out_shape=pltpu.VMEM((29, ATOMS, HALF), BF16),
            in_specs=[anywhere] * 5 + [pl.BlockSpec(memory_space=pltpu.SMEM)] + [anywhere] * 3,
            out_specs=in_vmem,
            scratch_shapes=[
                *[pltpu.VMEM((3, 4, 128), kind) for kind in (jnp.int32, jnp.int32, F32, F32)],
                pltpu.VMEM((3, 8, 128), jnp.int32),
                pltpu.VMEM(feats.shape, BF16),
                *[pltpu.VMEM((3, ATOMS, width), BF16) for width in WIDTH],
                pltpu.VMEM((3, 24, 128), F32),
                *[pltpu.VMEM((2, ATOMS, width), BF16) for width in WIDTH + WIDTH],
                pltpu.VMEM((2, 6, HALF, 768), BF16),
                pltpu.VMEM((2, 5, HALF, 640), BF16),
                pltpu.VMEM((7, HALF, 896), BF16),
                *[pltpu.VMEM((ATOMS, width), BF16) for width in GIVEN + GIVEN],
                dma((6,)), dma((4,)), dma((3,)), dma((3, 2)), dma((3, 2)), dma((2, 5)), dma((2, 5)),
                dma((3, 2)), dma((3, 2)), dma((3,)), dma((3,)),
            ],
            compiler_params=pltpu.CompilerParams(
                collective_id=0, has_side_effects=True, vmem_limit_bytes=60 * 1024 * 1024
            ),
            cost_estimate=pl.CostEstimate(
                flops=2 * 64 * 3 * 1024 * 1024, bytes_accessed=8 * 1024 * 1024, transcendentals=2048
            ),
            name="edge_mix",
        )(feats, source_index, target_index, edge_angle, edge_envelope, live_blocks,
          w_zero, w_one, w_two)
        return jnp.transpose(out, (1, 0, 2))

    return jax.shard_map(
        shards,
        mesh=mesh,
        in_specs=(
            P(("space", "help"), None, "chan"),
            P(("space", "help"), None),
            P(("space", "help"), None),
            P(("space", "help"), None),
            P(("space", "help"), None),
            P(("space", "help")),
            P(), P(), P(),
        ),
        out_specs=P(("space", "help"), None, "chan"),
        check_vma=False,
    )
```

```python
import functools

import jax
import jax.numpy as jnp
from jax import lax
from jax.experimental import pallas as pl
from jax.experimental.pallas import tpu as pltpu
from jax.sharding import PartitionSpec as P

MESH = pl.DeviceIdType.MESH
F32, BF16 = jnp.float32, jnp.bfloat16
ATOMS = 32
HALF = 64
ROW = 3 * ATOMS

PLUS_ONE = [l * l + l + 1 for l in range(1, 7)]
MINUS_ONE = [l * l + l - 1 for l in range(1, 7)]
PLUS_TWO = [l * l + l + 2 for l in range(2, 7)]
MINUS_TWO = [l * l + l - 2 for l in range(2, 7)]
ZERO = [l * l + l for l in range(7)]
PACK = (
    PLUS_ONE + MINUS_ONE,
    PLUS_TWO[:4] + MINUS_TWO[:4] + [PLUS_TWO[4], MINUS_TWO[4]],
    ZERO + ZERO[-1:],
)
WIDTH = tuple(HALF * len(order) for order in PACK)
RUNS = [(0, 4)] + [(l * l + l - 2, 5) for l in range(2, 7)]
OUT_AT = ((7, 12), (19, 10), (0, 7))
GIVEN = (768, 640, 512)
COS_ONE, SIN_ONE, COS_TWO, SIN_TWO, PLAIN = range(0, 20, 4)
FIRST = (0, 0, 0)


def dot(a, b):
    return jnp.dot(a, b, preferred_element_type=F32)


def kernel(
    n_space, n_help,
    x_hbm, src_hbm, tgt_hbm, ang_hbm, env_hbm, live_ref, w0_hbm, w1_hbm, w2_hbm,
    out_ref,
    src_ref, tgt_ref, ang_ref, env_ref, live_at, xv, rx_one, rx_two, rx_zero, edges,
    tx_one, tx_two, tx_zero, in_one, in_two, in_zero,
    wv_one, wv_two, wv_zero, give_one, give_two, give_zero, take_one, take_two, take_zero,
    x_sem, in_sem, w_sem, halo_send, halo_recv, edge_send, edge_recv,
    sum_send, sum_recv, out_send, out_recv,
):
    s, h, c = lax.axis_index("space"), lax.axis_index("help"), lax.axis_index("chan")
    has = ((h > 0, h < n_help - 1), (s > 0, s < n_space - 1))
    rx = (rx_one, rx_two, rx_zero)
    tx = (tx_one, tx_two, tx_zero)
    sums_in = (in_one, in_two, in_zero)
    give = (give_one, give_two, give_zero)
    take = (take_one, take_two, take_zero)
    partner = (s, h, 1 - c)

    def neighbour(axis, side):
        step = 2 * side - 1
        return (s, h + step, c) if axis == 0 else (s + step, h, c)

    barrier = pltpu.get_barrier_semaphore()

    def greet(device):
        pl.semaphore_signal(barrier, inc=1, device_id=device, device_id_type=MESH)

    greet(partner)
    expected = 1
    for axis in (1, 0):
        for side in (1, 0):
            expected = expected + has[axis][side].astype(jnp.int32)

            @pl.when(has[axis][side])
            def _():
                greet(neighbour(axis, side))

    x_loads = [
        pltpu.make_async_copy(x_hbm.at[pl.ds(*run)], xv.at[pl.ds(*run)], x_sem.at[at])
        for at, run in enumerate(RUNS)
    ]
    raw_hbm = (src_hbm, tgt_hbm, ang_hbm, env_hbm)
    raw = (src_ref, tgt_ref, ang_ref, env_ref, live_at)
    loads = [
        pltpu.make_async_copy(source, held.at[1], in_sem.at[at])
        for at, (source, held) in enumerate(zip(raw_hbm, raw))
    ]
    mine = pl.ds(pl.multiple_of(c * HALF, HALF), HALF)
    weights = [
        pltpu.make_async_copy(w1_hbm.at[:, :, mine], wv_one, w_sem.at[0]),
        pltpu.make_async_copy(w2_hbm.at[:, :, mine], wv_two, w_sem.at[1]),
        pltpu.make_async_copy(w0_hbm.at[:, mine], wv_zero, w_sem.at[2]),
    ]
    for load in x_loads + loads:
        load.start()

    live_at[1] = jnp.full((8, 128), live_ref[0], jnp.int32)

    def halo_copy(plane, side):
        return pltpu.make_async_remote_copy(
            src_ref=rx[plane].at[1], dst_ref=rx[plane].at[2 - 2 * side],
            send_sem=halo_send.at[plane, side], recv_sem=halo_recv.at[plane, 1 - side],
            device_id=neighbour(FIRST[plane], side), device_id_type=MESH,
        )

    def edge_copies(side):
        return [
            pltpu.make_async_remote_copy(
                src_ref=held.at[1] if at == 4 else raw_hbm[at], dst_ref=held.at[2 - 2 * side],
                send_sem=edge_send.at[side, at], recv_sem=edge_recv.at[1 - side, at],
                device_id=neighbour(1, side), device_id_type=MESH,
            )
            for at, held in enumerate(raw)
        ]

    def sum_copy(plane, side):
        return pltpu.make_async_remote_copy(
            src_ref=tx[plane].at[side], dst_ref=sums_in[plane].at[1 - side],
            send_sem=sum_send.at[plane, side], recv_sem=sum_recv.at[plane, 1 - side],
            device_id=neighbour(1 - FIRST[plane], side), device_id_type=MESH,
        )

    def out_copy(plane):
        return pltpu.make_async_remote_copy(
            src_ref=give[plane], dst_ref=take[plane],
            send_sem=out_send.at[plane], recv_sem=out_recv.at[plane],
            device_id=partner, device_id_type=MESH,
        )

    pl.semaphore_wait(barrier, expected)
    for side in range(2):

        @pl.when(has[1][side])
        def _():
            for copy in edge_copies(side):
                copy.start()

    for load in x_loads:
        load.wait()
    for plane, (ref, order) in enumerate(zip(rx, PACK)):
        for pair in range(len(order) // 2):
            ref[1, :, pl.ds(128 * pair, 128)] = jnp.concatenate(
                [xv[order[2 * pair]], xv[order[2 * pair + 1]]], axis=1
            )
        for side in range(2):

            @pl.when(has[FIRST[plane]][side])
            def _():
                halo_copy(plane, side).start()

    for load in weights:
        load.start()

    for axis in range(2):
        for side in range(2):

            @pl.when(jnp.logical_not(has[axis][side]))
            def _():
                if axis == 1:
                    for ref in raw:
                        ref[2 * side] = jnp.zeros(ref.shape[1:], ref.dtype)
                for plane in range(3):
                    if FIRST[plane] == axis:
                        rx[plane][2 * side] = jnp.zeros((ATOMS, WIDTH[plane]), BF16)
                    else:
                        sums_in[plane][side] = jnp.zeros((ATOMS, WIDTH[plane]), BF16)

    ids_row = lax.broadcasted_iota(jnp.int32, (ROW, 128), 0)
    ids_atom = lax.broadcasted_iota(jnp.int32, (ATOMS, 128), 0)
    block = lax.broadcasted_iota(jnp.int32, (4, 128), 0)

    def weigh(which):
        angle = ang_ref[which]
        cos, sin = jnp.cos(angle), jnp.sin(angle)
        alive = jnp.where(block < live_at[which, 0:4], env_ref[which], 0.0)
        for row, value in (
            (COS_ONE, alive * cos), (SIN_ONE, alive * sin),
            (COS_TWO, alive * ((cos - sin) * (cos + sin))), (SIN_TWO, alive * (2.0 * cos * sin)),
            (PLAIN, alive),
        ):
            edges[which, row:row + 4] = value

    def gathering(which):
        left, right = [], []
        for b in range(4):
            source = src_ref[which, b:b + 1] - ROW * (2 - which)
            target = tgt_ref[which, b:b + 1] == ids_atom
            right.append(jnp.where(source == ids_row, 1.0, 0.0).astype(BF16))
            left.append(jnp.concatenate([
                jnp.where(target, edges[which, at + b:at + b + 1], 0.0)
                for at in (COS_ONE, SIN_ONE, COS_TWO, SIN_TWO, PLAIN)
            ], axis=0).astype(BF16))
        return lax.dot_general(
            jnp.concatenate(left, axis=1), jnp.concatenate(right, axis=1),
            (((1,), (1,)), ((), ())), preferred_element_type=F32,
        ).astype(BF16)

    for load in loads:
        load.wait()
    weigh(1)
    middle = gathering(1)
    gathered = [None, middle, None]
    for side in (1, 0):

        @pl.when(has[1][side])
        def _():
            for copy in edge_copies(1 - side):
                copy.wait_recv()

        weigh(2 * side)
        gathered[2 * side] = gathering(2 * side)
    lhs = [
        jnp.concatenate([each[first:first + rows] for each in gathered], axis=0)
        for first, rows in ((0, 2 * ATOMS), (2 * ATOMS, 2 * ATOMS), (4 * ATOMS, ATOMS))
    ]
    low = lax.broadcasted_iota(jnp.int32, (ATOMS, 128), 1) < HALF

    def turned(plane, part):
        if plane == 2:
            return part
        by_cos, by_sin = part[:ATOMS], part[ATOMS:]
        if plane == 0:
            return jnp.concatenate([
                by_cos[:, :384] + by_sin[:, 384:], by_cos[:, 384:] - by_sin[:, :384]
            ], axis=1)
        crossed = pltpu.roll(by_sin[:, 512:], HALF, 1)
        return jnp.concatenate([
            by_cos[:, :256] + by_sin[:, 256:512],
            by_cos[:, 256:512] - by_sin[:, :256],
            by_cos[:, 512:] + jnp.where(low, crossed, -crossed),
        ], axis=1)

    own = []
    for plane in range(3):
        for side in range(2):

            @pl.when(has[FIRST[plane]][side])
            def _():
                halo_copy(plane, 1 - side).wait_recv()

        part = dot(lhs[plane], rx[plane][...].reshape(ROW, WIDTH[plane]))
        rows = part.shape[0] // 3
        for side in range(2):
            tx[plane][side] = turned(plane, part[2 * side * rows:(2 * side + 1) * rows]).astype(BF16)

            @pl.when(has[1 - FIRST[plane]][side])
            def _():
                sum_copy(plane, side).start()

        own.append(turned(plane, part[rows:2 * rows]))

    for axis in range(2):
        for side in range(2):

            @pl.when(has[axis][side])
            def _():
                if axis == 1:
                    for copy in edge_copies(side):
                        copy.wait_send()
                for plane in range(3):
                    if FIRST[plane] == axis:
                        halo_copy(plane, side).wait_send()

    for load in weights:
        load.wait()

    def by_lane(a, b):
        return (
            jnp.where(low, a, pltpu.roll(b, HALF, 1)),
            jnp.where(low, pltpu.roll(a, HALF, 1), b),
        )

    def rotated_mix(sums, real, imag):
        by_real, by_imag = dot(sums, real), dot(sums, imag)
        return [by_real[:ATOMS] - by_imag[ATOMS:], by_imag[:ATOMS] + by_real[ATOMS:]]

    first_core = c == 0
    kept = []
    for plane in range(3):
        for side in range(2):

            @pl.when(has[1 - FIRST[plane]][side])
            def _():
                sum_copy(plane, 1 - side).wait_recv()

        y = own[plane] + sums_in[plane][0].astype(F32) + sums_in[plane][1].astype(F32)
        if plane == 0:
            mixed = rotated_mix(
                jnp.concatenate([y[:, :384], y[:, 384:]], axis=0).astype(BF16),
                wv_one[0].reshape(384, 768), wv_one[1].reshape(384, 768),
            )
        elif plane == 1:
            tail = y[:, 512:]
            mixed = rotated_mix(
                jnp.concatenate([
                    jnp.concatenate([y[:, :256], tail], axis=1),
                    jnp.concatenate([y[:, 256:512], pltpu.roll(tail, HALF, 1)], axis=1),
                ], axis=0).astype(BF16)[:, :320],
                wv_two[0].reshape(320, 640), wv_two[1].reshape(320, 640),
            )
        else:
            mixed = [dot(y[:, :448].astype(BF16), wv_zero[...].reshape(448, 896))]
        blocks = [
            piece[:, 128 * degree:128 * degree + 128]
            for piece in mixed for degree in range(piece.shape[1] // 128)
        ]
        keep = []
        for pair in range((len(blocks) + 1) // 2):
            lower, upper = by_lane(blocks[2 * pair], blocks[min(2 * pair + 1, len(blocks) - 1)])
            keep.append(jnp.where(first_core, lower, upper))
            give[plane][:, pl.ds(128 * pair, 128)] = jnp.where(first_core, upper, lower).astype(BF16)
        kept.append(keep)
        out_copy(plane).start()

    for plane in range(3):
        for side in range(2):

            @pl.when(has[1 - FIRST[plane]][side])
            def _():
                sum_copy(plane, side).wait_send()

    for plane in range(3):
        out_copy(plane).wait_recv()
        row, count = OUT_AT[plane]
        for pair, keep in enumerate(kept[plane]):
            whole = (keep + take[plane][:, pl.ds(128 * pair, 128)].astype(F32)).astype(BF16)
            out_ref[row + 2 * pair] = whole[:, :HALF]
            if 2 * pair + 1 < count:
                out_ref[row + 2 * pair + 1] = whole[:, HALF:]

    for plane in range(3):
        out_copy(plane).wait_send()


def solution(mesh):
    n_space, n_help = mesh.shape["space"], mesh.shape["help"]

    def shards(node_feats, source_index, target_index, edge_angle, edge_envelope, live_blocks,
               w_zero, w_one, w_two):
        feats = jnp.transpose(node_feats, (1, 0, 2))
        anywhere = pl.BlockSpec(memory_space=pltpu.HBM)
        in_vmem = pl.BlockSpec(memory_space=pltpu.VMEM)
        dma = pltpu.SemaphoreType.DMA
        out = pl.pallas_call(
            functools.partial(kernel, n_space, n_help),
            out_shape=pltpu.VMEM((29, ATOMS, HALF), BF16),
            in_specs=[anywhere] * 5 + [pl.BlockSpec(memory_space=pltpu.SMEM)] + [anywhere] * 3,
            out_specs=in_vmem,
            scratch_shapes=[
                *[pltpu.VMEM((3, 4, 128), kind) for kind in (jnp.int32, jnp.int32, F32, F32)],
                pltpu.VMEM((3, 8, 128), jnp.int32),
                pltpu.VMEM(feats.shape, BF16),
                *[pltpu.VMEM((3, ATOMS, width), BF16) for width in WIDTH],
                pltpu.VMEM((3, 24, 128), F32),
                *[pltpu.VMEM((2, ATOMS, width), BF16) for width in WIDTH + WIDTH],
                pltpu.VMEM((2, 6, HALF, 768), BF16),
                pltpu.VMEM((2, 5, HALF, 640), BF16),
                pltpu.VMEM((7, HALF, 896), BF16),
                *[pltpu.VMEM((ATOMS, width), BF16) for width in GIVEN + GIVEN],
                dma((6,)), dma((4,)), dma((3,)), dma((3, 2)), dma((3, 2)), dma((2, 5)), dma((2, 5)),
                dma((3, 2)), dma((3, 2)), dma((3,)), dma((3,)),
            ],
            compiler_params=pltpu.CompilerParams(
                collective_id=0, has_side_effects=True, vmem_limit_bytes=60 * 1024 * 1024
            ),
            cost_estimate=pl.CostEstimate(
                flops=2 * 64 * 3 * 1024 * 1024, bytes_accessed=8 * 1024 * 1024, transcendentals=2048
            ),
            name="edge_mix",
        )(feats, source_index, target_index, edge_angle, edge_envelope, live_blocks,
          w_zero, w_one, w_two)
        return jnp.transpose(out, (1, 0, 2))

    return jax.shard_map(
        shards,
        mesh=mesh,
        in_specs=(
            P(("space", "help"), None, "chan"),
            P(("space", "help"), None),
            P(("space", "help"), None),
            P(("space", "help"), None),
            P(("space", "help"), None),
            P(("space", "help")),
            P(), P(), P(),
        ),
        out_specs=P(("space", "help"), None, "chan"),
        check_vma=False,
    )
```

```python
import functools

import jax
import jax.numpy as jnp
from jax import lax
from jax.experimental import pallas as pl
from jax.experimental.pallas import tpu as pltpu
from jax.sharding import PartitionSpec as P

MESH = pl.DeviceIdType.MESH
F32, BF16 = jnp.float32, jnp.bfloat16
ATOMS = 32
HALF = 64
ROW = 3 * ATOMS

PLUS_ONE = [l * l + l + 1 for l in range(1, 7)]
MINUS_ONE = [l * l + l - 1 for l in range(1, 7)]
PLUS_TWO = [l * l + l + 2 for l in range(2, 7)]
MINUS_TWO = [l * l + l - 2 for l in range(2, 7)]
ZERO = [l * l + l for l in range(7)]
PACK = (
    PLUS_ONE + MINUS_ONE,
    PLUS_TWO[:4] + MINUS_TWO[:4] + [PLUS_TWO[4], MINUS_TWO[4]],
    ZERO + ZERO[-1:],
)
WIDTH = tuple(HALF * len(order) for order in PACK)
RUNS = [(0, 4)] + [(l * l + l - 2, 5) for l in range(2, 7)]
OUT_AT = ((7, 12), (19, 10), (0, 7))
GIVEN = (768, 640, 512)
COS_ONE, SIN_ONE, COS_TWO, SIN_TWO, PLAIN = range(0, 20, 4)
FIRST = (0, 0, 0)


def dot(a, b):
    return jnp.dot(a, b, preferred_element_type=F32)


def kernel(
    n_space, n_help,
    x_hbm, src_hbm, tgt_hbm, ang_hbm, env_hbm, live_ref, w0_hbm, w1_hbm, w2_hbm,
    out_ref,
    src_ref, tgt_ref, ang_ref, env_ref, live_at, xv, rx_one, rx_rest, edges,
    tx_one, tx_rest, in_one, in_rest,
    wv_one, wv_two, wv_zero, give_one, give_two, give_zero, take_one, take_two, take_zero,
    x_sem, in_sem, w_sem, halo_send, halo_recv, edge_send, edge_recv,
    sum_send, sum_recv, out_send, out_recv,
):
    s, h, c = lax.axis_index("space"), lax.axis_index("help"), lax.axis_index("chan")
    has = ((h > 0, h < n_help - 1), (s > 0, s < n_space - 1))
    rx_groups, tx_groups, in_groups = (rx_one, rx_rest), (tx_one, tx_rest), (in_one, in_rest)

    def planes(one, rest):
        return one, rest.at[:, :, 0:WIDTH[1]], rest.at[:, :, WIDTH[1]:WIDTH[1] + WIDTH[2]]

    rx, tx, sums_in = planes(*rx_groups), planes(*tx_groups), planes(*in_groups)
    give = (give_one, give_two, give_zero)
    take = (take_one, take_two, take_zero)
    partner = (s, h, 1 - c)

    def neighbour(axis, side):
        step = 2 * side - 1
        return (s, h + step, c) if axis == 0 else (s + step, h, c)

    barrier = pltpu.get_barrier_semaphore()

    def greet(device):
        pl.semaphore_signal(barrier, inc=1, device_id=device, device_id_type=MESH)

    greet(partner)
    expected = 1
    for axis in (1, 0):
        for side in (1, 0):
            expected = expected + has[axis][side].astype(jnp.int32)

            @pl.when(has[axis][side])
            def _():
                greet(neighbour(axis, side))

    x_loads = [
        pltpu.make_async_copy(x_hbm.at[pl.ds(*run)], xv.at[pl.ds(*run)], x_sem.at[at])
        for at, run in enumerate(RUNS)
    ]
    raw_hbm = (src_hbm, tgt_hbm, ang_hbm, env_hbm)
    raw = (src_ref, tgt_ref, ang_ref, env_ref, live_at)
    loads = [
        pltpu.make_async_copy(source, held.at[1], in_sem.at[at])
        for at, (source, held) in enumerate(zip(raw_hbm, raw))
    ]
    mine = pl.ds(pl.multiple_of(c * HALF, HALF), HALF)
    weights = [
        pltpu.make_async_copy(w1_hbm.at[:, :, mine], wv_one, w_sem.at[0]),
        pltpu.make_async_copy(w2_hbm.at[:, :, mine], wv_two, w_sem.at[1]),
        pltpu.make_async_copy(w0_hbm.at[:, mine], wv_zero, w_sem.at[2]),
    ]
    for load in x_loads + loads:
        load.start()

    live_at[1] = jnp.full((8, 128), live_ref[0], jnp.int32)

    def halo_copy(plane, side):
        return pltpu.make_async_remote_copy(
            src_ref=rx_groups[plane].at[1], dst_ref=rx_groups[plane].at[2 - 2 * side],
            send_sem=halo_send.at[plane, side], recv_sem=halo_recv.at[plane, 1 - side],
            device_id=neighbour(FIRST[plane], side), device_id_type=MESH,
        )

    def edge_copies(side):
        return [
            pltpu.make_async_remote_copy(
                src_ref=held.at[1] if at == 4 else raw_hbm[at], dst_ref=held.at[2 - 2 * side],
                send_sem=edge_send.at[side, at], recv_sem=edge_recv.at[1 - side, at],
                device_id=neighbour(1, side), device_id_type=MESH,
            )
            for at, held in enumerate(raw)
        ]

    def sum_copy(plane, side):
        return pltpu.make_async_remote_copy(
            src_ref=tx_groups[plane].at[side], dst_ref=in_groups[plane].at[1 - side],
            send_sem=sum_send.at[plane, side], recv_sem=sum_recv.at[plane, 1 - side],
            device_id=neighbour(1 - FIRST[plane], side), device_id_type=MESH,
        )

    def out_copy(plane):
        return pltpu.make_async_remote_copy(
            src_ref=give[plane], dst_ref=take[plane],
            send_sem=out_send.at[plane], recv_sem=out_recv.at[plane],
            device_id=partner, device_id_type=MESH,
        )

    pl.semaphore_wait(barrier, expected)
    for side in range(2):

        @pl.when(has[1][side])
        def _():
            for copy in edge_copies(side):
                copy.start()

    for load in x_loads:
        load.wait()
    for plane, (ref, order) in enumerate(zip(rx, PACK)):
        for pair in range(len(order) // 2):
            ref[1, :, pl.ds(128 * pair, 128)] = jnp.concatenate(
                [xv[order[2 * pair]], xv[order[2 * pair + 1]]], axis=1
            )
        for side in range(2) if plane != 1 else ():

            @pl.when(has[FIRST[plane]][side])
            def _():
                halo_copy(min(plane, 1), side).start()

    for load in weights:
        load.start()

    for axis in range(2):
        for side in range(2):

            @pl.when(jnp.logical_not(has[axis][side]))
            def _():
                if axis == 1:
                    for ref in raw:
                        ref[2 * side] = jnp.zeros(ref.shape[1:], ref.dtype)
                for plane in range(3):
                    if FIRST[plane] == axis:
                        rx[plane][2 * side] = jnp.zeros((ATOMS, WIDTH[plane]), BF16)
                    else:
                        sums_in[plane][side] = jnp.zeros((ATOMS, WIDTH[plane]), BF16)

    ids_row = lax.broadcasted_iota(jnp.int32, (ROW, 128), 0)
    ids_atom = lax.broadcasted_iota(jnp.int32, (ATOMS, 128), 0)
    block = lax.broadcasted_iota(jnp.int32, (4, 128), 0)

    def weigh(which):
        angle = ang_ref[which]
        cos, sin = jnp.cos(angle), jnp.sin(angle)
        alive = jnp.where(block < live_at[which, 0:4], env_ref[which], 0.0)
        for row, value in (
            (COS_ONE, alive * cos), (SIN_ONE, alive * sin),
            (COS_TWO, alive * ((cos - sin) * (cos + sin))), (SIN_TWO, alive * (2.0 * cos * sin)),
            (PLAIN, alive),
        ):
            edges[which, row:row + 4] = value

    def gathering(which):
        left, right = [], []
        for b in range(4):
            source = src_ref[which, b:b + 1] - ROW * (2 - which)
            target = tgt_ref[which, b:b + 1] == ids_atom
            right.append(jnp.where(source == ids_row, 1.0, 0.0).astype(BF16))
            left.append(jnp.concatenate([
                jnp.where(target, edges[which, at + b:at + b + 1], 0.0)
                for at in (COS_ONE, SIN_ONE, COS_TWO, SIN_TWO, PLAIN)
            ], axis=0).astype(BF16))
        return lax.dot_general(
            jnp.concatenate(left, axis=1), jnp.concatenate(right, axis=1),
            (((1,), (1,)), ((), ())), preferred_element_type=F32,
        ).astype(BF16)

    for load in loads:
        load.wait()
    weigh(1)
    middle = gathering(1)
    gathered = [None, middle, None]
    for side in (1, 0):

        @pl.when(has[1][side])
        def _():
            for copy in edge_copies(1 - side):
                copy.wait_recv()

        weigh(2 * side)
        gathered[2 * side] = gathering(2 * side)
    lhs = [
        jnp.concatenate([each[first:first + rows] for each in gathered], axis=0)
        for first, rows in ((0, 2 * ATOMS), (2 * ATOMS, 2 * ATOMS), (4 * ATOMS, ATOMS))
    ]
    low = lax.broadcasted_iota(jnp.int32, (ATOMS, 128), 1) < HALF

    def turned(plane, part):
        if plane == 2:
            return part
        by_cos, by_sin = part[:ATOMS], part[ATOMS:]
        if plane == 0:
            return jnp.concatenate([
                by_cos[:, :384] + by_sin[:, 384:], by_cos[:, 384:] - by_sin[:, :384]
            ], axis=1)
        crossed = pltpu.roll(by_sin[:, 512:], HALF, 1)
        return jnp.concatenate([
            by_cos[:, :256] + by_sin[:, 256:512],
            by_cos[:, 256:512] - by_sin[:, :256],
            by_cos[:, 512:] + jnp.where(low, crossed, -crossed),
        ], axis=1)

    own = []
    for plane in range(3):
        for side in range(2) if plane != 2 else ():

            @pl.when(has[FIRST[plane]][side])
            def _():
                halo_copy(plane, 1 - side).wait_recv()

        part = dot(lhs[plane], rx[plane][...].reshape(ROW, WIDTH[plane]))
        rows = part.shape[0] // 3
        for side in range(2):
            tx[plane][side] = turned(plane, part[2 * side * rows:(2 * side + 1) * rows]).astype(BF16)

            if plane != 1:

                @pl.when(has[1 - FIRST[plane]][side])
                def _():
                    sum_copy(min(plane, 1), side).start()

        own.append(turned(plane, part[rows:2 * rows]))

    for axis in range(2):
        for side in range(2):

            @pl.when(has[axis][side])
            def _():
                if axis == 1:
                    for copy in edge_copies(side):
                        copy.wait_send()
                for plane in range(2):
                    if FIRST[plane] == axis:
                        halo_copy(plane, side).wait_send()

    for load in weights:
        load.wait()

    def by_lane(a, b):
        return (
            jnp.where(low, a, pltpu.roll(b, HALF, 1)),
            jnp.where(low, pltpu.roll(a, HALF, 1), b),
        )

    def rotated_mix(sums, real, imag):
        by_real, by_imag = dot(sums, real), dot(sums, imag)
        return [by_real[:ATOMS] - by_imag[ATOMS:], by_imag[:ATOMS] + by_real[ATOMS:]]

    first_core = c == 0
    kept = []
    for plane in range(3):
        for side in range(2) if plane != 2 else ():

            @pl.when(has[1 - FIRST[plane]][side])
            def _():
                sum_copy(plane, 1 - side).wait_recv()

        y = own[plane] + sums_in[plane][0].astype(F32) + sums_in[plane][1].astype(F32)
        if plane == 0:
            mixed = rotated_mix(
                jnp.concatenate([y[:, :384], y[:, 384:]], axis=0).astype(BF16),
                wv_one[0].reshape(384, 768), wv_one[1].reshape(384, 768),
            )
        elif plane == 1:
            tail = y[:, 512:]
            mixed = rotated_mix(
                jnp.concatenate([
                    jnp.concatenate([y[:, :256], tail], axis=1),
                    jnp.concatenate([y[:, 256:512], pltpu.roll(tail, HALF, 1)], axis=1),
                ], axis=0).astype(BF16)[:, :320],
                wv_two[0].reshape(320, 640), wv_two[1].reshape(320, 640),
            )
        else:
            mixed = [dot(y[:, :448].astype(BF16), wv_zero[...].reshape(448, 896))]
        blocks = [
            piece[:, 128 * degree:128 * degree + 128]
            for piece in mixed for degree in range(piece.shape[1] // 128)
        ]
        keep = []
        for pair in range((len(blocks) + 1) // 2):
            lower, upper = by_lane(blocks[2 * pair], blocks[min(2 * pair + 1, len(blocks) - 1)])
            keep.append(jnp.where(first_core, lower, upper))
            give[plane][:, pl.ds(128 * pair, 128)] = jnp.where(first_core, upper, lower).astype(BF16)
        kept.append(keep)
        out_copy(plane).start()

    for plane in range(2):
        for side in range(2):

            @pl.when(has[1 - FIRST[plane]][side])
            def _():
                sum_copy(plane, side).wait_send()

    for plane in range(3):
        out_copy(plane).wait_recv()
        row, count = OUT_AT[plane]
        for pair, keep in enumerate(kept[plane]):
            whole = (keep + take[plane][:, pl.ds(128 * pair, 128)].astype(F32)).astype(BF16)
            out_ref[row + 2 * pair] = whole[:, :HALF]
            if 2 * pair + 1 < count:
                out_ref[row + 2 * pair + 1] = whole[:, HALF:]

    for plane in range(3):
        out_copy(plane).wait_send()


def solution(mesh):
    n_space, n_help = mesh.shape["space"], mesh.shape["help"]

    def shards(node_feats, source_index, target_index, edge_angle, edge_envelope, live_blocks,
               w_zero, w_one, w_two):
        feats = jnp.transpose(node_feats, (1, 0, 2))
        anywhere = pl.BlockSpec(memory_space=pltpu.HBM)
        in_vmem = pl.BlockSpec(memory_space=pltpu.VMEM)
        dma = pltpu.SemaphoreType.DMA
        out = pl.pallas_call(
            functools.partial(kernel, n_space, n_help),
            out_shape=pltpu.VMEM((29, ATOMS, HALF), BF16),
            in_specs=[anywhere] * 5 + [pl.BlockSpec(memory_space=pltpu.SMEM)] + [anywhere] * 3,
            out_specs=in_vmem,
            scratch_shapes=[
                *[pltpu.VMEM((3, 4, 128), kind) for kind in (jnp.int32, jnp.int32, F32, F32)],
                pltpu.VMEM((3, 8, 128), jnp.int32),
                pltpu.VMEM(feats.shape, BF16),
                *[pltpu.VMEM((3, ATOMS, width), BF16) for width in (WIDTH[0], WIDTH[1] + WIDTH[2])],
                pltpu.VMEM((3, 24, 128), F32),
                *[pltpu.VMEM((2, ATOMS, width), BF16) for width in 2 * (WIDTH[0], WIDTH[1] + WIDTH[2])],
                pltpu.VMEM((2, 6, HALF, 768), BF16),
                pltpu.VMEM((2, 5, HALF, 640), BF16),
                pltpu.VMEM((7, HALF, 896), BF16),
                *[pltpu.VMEM((ATOMS, width), BF16) for width in GIVEN + GIVEN],
                dma((6,)), dma((4,)), dma((3,)), dma((2, 2)), dma((2, 2)), dma((2, 5)), dma((2, 5)),
                dma((2, 2)), dma((2, 2)), dma((3,)), dma((3,)),
            ],
            compiler_params=pltpu.CompilerParams(
                collective_id=0, has_side_effects=True, vmem_limit_bytes=60 * 1024 * 1024
            ),
            cost_estimate=pl.CostEstimate(
                flops=2 * 64 * 3 * 1024 * 1024, bytes_accessed=8 * 1024 * 1024, transcendentals=2048
            ),
            name="edge_mix",
        )(feats, source_index, target_index, edge_angle, edge_envelope, live_blocks,
          w_zero, w_one, w_two)
        return jnp.transpose(out, (1, 0, 2))

    return jax.shard_map(
        shards,
        mesh=mesh,
        in_specs=(
            P(("space", "help"), None, "chan"),
            P(("space", "help"), None),
            P(("space", "help"), None),
            P(("space", "help"), None),
            P(("space", "help"), None),
            P(("space", "help")),
            P(), P(), P(),
        ),
        out_specs=P(("space", "help"), None, "chan"),
        check_vma=False,
    )
```

```python
import functools

import jax
import jax.numpy as jnp
from jax import lax
from jax.experimental import pallas as pl
from jax.experimental.pallas import tpu as pltpu
from jax.sharding import PartitionSpec as P

MESH = pl.DeviceIdType.MESH
F32, BF16 = jnp.float32, jnp.bfloat16
ATOMS = 32
HALF = 64
ROW = 3 * ATOMS

PLUS_ONE = [l * l + l + 1 for l in range(1, 7)]
MINUS_ONE = [l * l + l - 1 for l in range(1, 7)]
PLUS_TWO = [l * l + l + 2 for l in range(2, 7)]
MINUS_TWO = [l * l + l - 2 for l in range(2, 7)]
ZERO = [l * l + l for l in range(7)]
PACK = (
    PLUS_ONE + MINUS_ONE,
    PLUS_TWO[:4] + MINUS_TWO[:4] + [PLUS_TWO[4], MINUS_TWO[4]],
    ZERO + ZERO[-1:],
)
WIDTH = tuple(HALF * len(order) for order in PACK)
RUNS = [(0, 4)] + [(l * l + l - 2, 5) for l in range(2, 7)]
OUT_AT = ((7, 12), (19, 10), (0, 7))
GIVEN = (768, 640, 512)
COS_ONE, SIN_ONE, COS_TWO, SIN_TWO, PLAIN = range(0, 20, 4)
FIRST = (0, 0, 0)


def dot(a, b):
    return jnp.dot(a, b, preferred_element_type=F32)


def kernel(
    n_space, n_help,
    x_hbm, src_hbm, tgt_hbm, ang_hbm, env_hbm, live_ref, w0_hbm, w1_hbm, w2_hbm,
    out_ref,
    src_ref, tgt_ref, ang_ref, env_ref, live_at, xv, rx_one, rx_two, rx_zero, edges,
    tx_one, tx_two, tx_zero, in_one, in_two, in_zero,
    wv_one, wv_two, wv_zero, give_one, give_two, give_zero, take_one, take_two, take_zero,
    x_sem, in_sem, w_sem, halo_send, halo_recv, edge_send, edge_recv,
    sum_send, sum_recv, out_send, out_recv,
):
    s, h, c = lax.axis_index("space"), lax.axis_index("help"), lax.axis_index("chan")
    has = ((h > 0, h < n_help - 1), (s > 0, s < n_space - 1))
    rx = (rx_one, rx_two, rx_zero)
    tx = (tx_one, tx_two, tx_zero)
    sums_in = (in_one, in_two, in_zero)
    give = (give_one, give_two, give_zero)
    take = (take_one, take_two, take_zero)
    partner = (s, h, 1 - c)

    def neighbour(axis, side):
        step = 2 * side - 1
        return (s, h + step, c) if axis == 0 else (s + step, h, c)

    barrier = pltpu.get_barrier_semaphore()

    def greet(device):
        pl.semaphore_signal(barrier, inc=1, device_id=device, device_id_type=MESH)

    greet(partner)
    expected = 1
    for axis in (1, 0):
        for side in (1, 0):
            expected = expected + has[axis][side].astype(jnp.int32)

            @pl.when(has[axis][side])
            def _():
                greet(neighbour(axis, side))

    x_loads = [
        pltpu.make_async_copy(x_hbm.at[pl.ds(*run)], xv.at[pl.ds(*run)], x_sem.at[at])
        for at, run in enumerate(RUNS)
    ]
    raw_hbm = (src_hbm, tgt_hbm, ang_hbm, env_hbm)
    raw = (src_ref, tgt_ref, ang_ref, env_ref, live_at)
    loads = [
        pltpu.make_async_copy(source, held.at[1], in_sem.at[at])
        for at, (source, held) in enumerate(zip(raw_hbm, raw))
    ]
    mine = pl.ds(pl.multiple_of(c * HALF, HALF), HALF)
    weights = [
        pltpu.make_async_copy(w1_hbm.at[:, :, mine], wv_one, w_sem.at[0]),
        pltpu.make_async_copy(w2_hbm.at[:, :, mine], wv_two, w_sem.at[1]),
        pltpu.make_async_copy(w0_hbm.at[:, mine], wv_zero, w_sem.at[2]),
    ]
    for load in x_loads + loads:
        load.start()

    live_at[1] = jnp.full((8, 128), live_ref[0], jnp.int32)

    def halo_copy(plane, side):
        return pltpu.make_async_remote_copy(
            src_ref=rx[plane].at[1], dst_ref=rx[plane].at[2 - 2 * side],
            send_sem=halo_send.at[plane, side], recv_sem=halo_recv.at[plane, 1 - side],
            device_id=neighbour(FIRST[plane], side), device_id_type=MESH,
        )

    def edge_copies(side):
        return [
            pltpu.make_async_remote_copy(
                src_ref=held.at[1] if at == 4 else raw_hbm[at], dst_ref=held.at[2 - 2 * side],
                send_sem=edge_send.at[side, at], recv_sem=edge_recv.at[1 - side, at],
                device_id=neighbour(1, side), device_id_type=MESH,
            )
            for at, held in enumerate(raw)
        ]

    def sum_copy(plane, side):
        return pltpu.make_async_remote_copy(
            src_ref=tx[plane].at[side], dst_ref=sums_in[plane].at[1 - side],
            send_sem=sum_send.at[plane, side], recv_sem=sum_recv.at[plane, 1 - side],
            device_id=neighbour(1 - FIRST[plane], side), device_id_type=MESH,
        )

    def out_copy(plane):
        return pltpu.make_async_remote_copy(
            src_ref=give[plane], dst_ref=take[plane],
            send_sem=out_send.at[plane], recv_sem=out_recv.at[plane],
            device_id=partner, device_id_type=MESH,
        )

    pl.semaphore_wait(barrier, expected)
    for side in range(2):

        @pl.when(has[1][side])
        def _():
            for copy in edge_copies(side):
                copy.start()

    for load in x_loads:
        load.wait()
    for plane, (ref, order) in enumerate(zip(rx, PACK)):
        for pair in range(len(order) // 2):
            ref[1, :, pl.ds(128 * pair, 128)] = jnp.concatenate(
                [xv[order[2 * pair]], xv[order[2 * pair + 1]]], axis=1
            )
        for side in range(2):

            @pl.when(has[FIRST[plane]][side])
            def _():
                halo_copy(plane, side).start()

    for load in weights:
        load.start()

    for axis in range(2):
        for side in range(2):

            @pl.when(jnp.logical_not(has[axis][side]))
            def _():
                if axis == 1:
                    for ref in raw:
                        ref[2 * side] = jnp.zeros(ref.shape[1:], ref.dtype)
                for plane in range(3):
                    if FIRST[plane] == axis:
                        rx[plane][2 * side] = jnp.zeros((ATOMS, WIDTH[plane]), BF16)
                    else:
                        sums_in[plane][side] = jnp.zeros((ATOMS, WIDTH[plane]), BF16)

    ids_row = lax.broadcasted_iota(jnp.int32, (ROW, 128), 0)
    ids_atom = lax.broadcasted_iota(jnp.int32, (ATOMS, 128), 0)
    block = lax.broadcasted_iota(jnp.int32, (4, 128), 0)

    def weigh(which):
        angle = ang_ref[which]
        cos, sin = jnp.cos(angle), jnp.sin(angle)
        alive = jnp.where(block < live_at[which, 0:4], env_ref[which], 0.0)
        for row, value in (
            (COS_ONE, alive * cos), (SIN_ONE, alive * sin),
            (COS_TWO, alive * ((cos - sin) * (cos + sin))), (SIN_TWO, alive * (2.0 * cos * sin)),
            (PLAIN, alive),
        ):
            edges[which, row:row + 4] = value

    def gathering(which):
        left, right = [], []
        for b in range(4):
            source = src_ref[which, b:b + 1] - ROW * (2 - which)
            target = tgt_ref[which, b:b + 1] == ids_atom
            right.append(jnp.where(source == ids_row, 1.0, 0.0).astype(BF16))
            left.append(jnp.concatenate([
                jnp.where(target, edges[which, at + b:at + b + 1], 0.0)
                for at in (COS_ONE, SIN_ONE, COS_TWO, SIN_TWO, PLAIN)
            ], axis=0).astype(BF16))
        return lax.dot_general(
            jnp.concatenate(left, axis=1), jnp.concatenate(right, axis=1),
            (((1,), (1,)), ((), ())), preferred_element_type=F32,
        ).astype(BF16)

    for load in loads:
        load.wait()
    weigh(1)
    middle = gathering(1)
    gathered = [None, middle, None]
    for side in (1, 0):

        @pl.when(has[1][side])
        def _():
            for copy in edge_copies(1 - side):
                copy.wait_recv()

        weigh(2 * side)
        gathered[2 * side] = gathering(2 * side)
    lhs = [
        jnp.concatenate([each[first:first + rows] for each in gathered], axis=0)
        for first, rows in ((0, 2 * ATOMS), (2 * ATOMS, 2 * ATOMS), (4 * ATOMS, ATOMS))
    ]
    low = lax.broadcasted_iota(jnp.int32, (ATOMS, 128), 1) < HALF

    def turned(plane, part):
        if plane == 2:
            return part
        by_cos, by_sin = part[:ATOMS], part[ATOMS:]
        if plane == 0:
            return jnp.concatenate([
                by_cos[:, :384] + by_sin[:, 384:], by_cos[:, 384:] - by_sin[:, :384]
            ], axis=1)
        crossed = pltpu.roll(by_sin[:, 512:], HALF, 1)
        return jnp.concatenate([
            by_cos[:, :256] + by_sin[:, 256:512],
            by_cos[:, 256:512] - by_sin[:, :256],
            by_cos[:, 512:] + jnp.where(low, crossed, -crossed),
        ], axis=1)

    own = []
    for plane in range(3):
        for side in range(2):

            @pl.when(has[FIRST[plane]][side])
            def _():
                halo_copy(plane, 1 - side).wait_recv()

        part = dot(lhs[plane], rx[plane][...].reshape(ROW, WIDTH[plane]))
        rows = part.shape[0] // 3
        for side in range(2):
            tx[plane][side] = turned(plane, part[2 * side * rows:(2 * side + 1) * rows]).astype(BF16)

            @pl.when(has[1 - FIRST[plane]][side])
            def _():
                sum_copy(plane, side).start()

        own.append(part[rows:2 * rows])
    own = [turned(plane, part) for plane, part in enumerate(own)]

    for axis in range(2):
        for side in range(2):

            @pl.when(has[axis][side])
            def _():
                if axis == 1:
                    for copy in edge_copies(side):
                        copy.wait_send()
                for plane in range(3):
                    if FIRST[plane] == axis:
                        halo_copy(plane, side).wait_send()

    for load in weights:
        load.wait()

    def by_lane(a, b):
        return (
            jnp.where(low, a, pltpu.roll(b, HALF, 1)),
            jnp.where(low, pltpu.roll(a, HALF, 1), b),
        )

    def rotated_mix(sums, real, imag):
        by_real, by_imag = dot(sums, real), dot(sums, imag)
        return [by_real[:ATOMS] - by_imag[ATOMS:], by_imag[:ATOMS] + by_real[ATOMS:]]

    first_core = c == 0
    kept = []
    for plane in range(3):
        for side in range(2):

            @pl.when(has[1 - FIRST[plane]][side])
            def _():
                sum_copy(plane, 1 - side).wait_recv()

        y = own[plane] + sums_in[plane][0].astype(F32) + sums_in[plane][1].astype(F32)
        if plane == 0:
            mixed = rotated_mix(
                jnp.concatenate([y[:, :384], y[:, 384:]], axis=0).astype(BF16),
                wv_one[0].reshape(384, 768), wv_one[1].reshape(384, 768),
            )
        elif plane == 1:
            tail = y[:, 512:]
            mixed = rotated_mix(
                jnp.concatenate([
                    jnp.concatenate([y[:, :256], tail], axis=1),
                    jnp.concatenate([y[:, 256:512], pltpu.roll(tail, HALF, 1)], axis=1),
                ], axis=0).astype(BF16)[:, :320],
                wv_two[0].reshape(320, 640), wv_two[1].reshape(320, 640),
            )
        else:
            mixed = [dot(y[:, :448].astype(BF16), wv_zero[...].reshape(448, 896))]
        blocks = [
            piece[:, 128 * degree:128 * degree + 128]
            for piece in mixed for degree in range(piece.shape[1] // 128)
        ]
        keep = []
        for pair in range((len(blocks) + 1) // 2):
            lower, upper = by_lane(blocks[2 * pair], blocks[min(2 * pair + 1, len(blocks) - 1)])
            keep.append(jnp.where(first_core, lower, upper))
            give[plane][:, pl.ds(128 * pair, 128)] = jnp.where(first_core, upper, lower).astype(BF16)
        kept.append(keep)
        out_copy(plane).start()

    for plane in range(3):
        for side in range(2):

            @pl.when(has[1 - FIRST[plane]][side])
            def _():
                sum_copy(plane, side).wait_send()

    for plane in range(3):
        out_copy(plane).wait_recv()
        row, count = OUT_AT[plane]
        for pair, keep in enumerate(kept[plane]):
            whole = (keep + take[plane][:, pl.ds(128 * pair, 128)].astype(F32)).astype(BF16)
            out_ref[row + 2 * pair] = whole[:, :HALF]
            if 2 * pair + 1 < count:
                out_ref[row + 2 * pair + 1] = whole[:, HALF:]

    for plane in range(3):
        out_copy(plane).wait_send()


def solution(mesh):
    n_space, n_help = mesh.shape["space"], mesh.shape["help"]

    def shards(node_feats, source_index, target_index, edge_angle, edge_envelope, live_blocks,
               w_zero, w_one, w_two):
        feats = jnp.transpose(node_feats, (1, 0, 2))
        anywhere = pl.BlockSpec(memory_space=pltpu.HBM)
        in_vmem = pl.BlockSpec(memory_space=pltpu.VMEM)
        dma = pltpu.SemaphoreType.DMA
        out = pl.pallas_call(
            functools.partial(kernel, n_space, n_help),
            out_shape=pltpu.VMEM((29, ATOMS, HALF), BF16),
            in_specs=[anywhere] * 5 + [pl.BlockSpec(memory_space=pltpu.SMEM)] + [anywhere] * 3,
            out_specs=in_vmem,
            scratch_shapes=[
                *[pltpu.VMEM((3, 4, 128), kind) for kind in (jnp.int32, jnp.int32, F32, F32)],
                pltpu.VMEM((3, 8, 128), jnp.int32),
                pltpu.VMEM(feats.shape, BF16),
                *[pltpu.VMEM((3, ATOMS, width), BF16) for width in WIDTH],
                pltpu.VMEM((3, 24, 128), F32),
                *[pltpu.VMEM((2, ATOMS, width), BF16) for width in WIDTH + WIDTH],
                pltpu.VMEM((2, 6, HALF, 768), BF16),
                pltpu.VMEM((2, 5, HALF, 640), BF16),
                pltpu.VMEM((7, HALF, 896), BF16),
                *[pltpu.VMEM((ATOMS, width), BF16) for width in GIVEN + GIVEN],
                dma((6,)), dma((4,)), dma((3,)), dma((3, 2)), dma((3, 2)), dma((2, 5)), dma((2, 5)),
                dma((3, 2)), dma((3, 2)), dma((3,)), dma((3,)),
            ],
            compiler_params=pltpu.CompilerParams(
                collective_id=0, has_side_effects=True, vmem_limit_bytes=60 * 1024 * 1024
            ),
            cost_estimate=pl.CostEstimate(
                flops=2 * 64 * 3 * 1024 * 1024, bytes_accessed=8 * 1024 * 1024, transcendentals=2048
            ),
            name="edge_mix",
        )(feats, source_index, target_index, edge_angle, edge_envelope, live_blocks,
          w_zero, w_one, w_two)
        return jnp.transpose(out, (1, 0, 2))

    return jax.shard_map(
        shards,
        mesh=mesh,
        in_specs=(
            P(("space", "help"), None, "chan"),
            P(("space", "help"), None),
            P(("space", "help"), None),
            P(("space", "help"), None),
            P(("space", "help"), None),
            P(("space", "help")),
            P(), P(), P(),
        ),
        out_specs=P(("space", "help"), None, "chan"),
        check_vma=False,
    )
```
